32 devices in a mesh: groups: 2 (over x), dp: 8 (over z, y), tensor: 2 (over core).
Axes of the slice: x: 2, y: 2, z: 4, core: 2. Of those that a mesh axis runs over, the one named last changes fastest.
Arguments:
- step_hidden: bfloat16 [16, 32, 64, 4096], P('dp', 'groups', None, 'tensor'), parts along dimension 1, may hold values from -80 to 80
- prm_gain: float32 [4096], P('tensor'), may hold values from 0.1 to 1.9
- score_weight: float32 [4096], P('tensor'), may hold values from -0.09375 to 0.09375
- step_bounds: int32 [16, 32], P('dp', 'groups'), parts along dimension 1, may hold values from 0 to 63
- queries: bfloat16 [16, 32, 8192], P('dp', 'groups', 'tensor'), parts along dimension 1, may hold values from -16 to 16
- step_kv: bfloat16 [16, 32, 2, 64, 1024], P('dp', 'groups', None, None, 'tensor'), parts along dimension 1, may hold values from -4 to 4
- caches: bfloat16 [16, 32, 2, 128, 1024], P('dp', 'groups', None, None, 'tensor'), parts along dimension 1, may hold values from -4 to 4
- parents: int32 [16, 32, 1], P(None, 'groups'), parts along dimension 1, may hold values from 0 to 15; in each aligned block of 16 rows (0 to 15, 16 to 31, ..., all dimensions but the last counted through in order) at most 3 rows name the same one
- lengths: int32 [16, 32], P(None, 'groups'), parts along dimension 1, may hold values from 16 to 128
Outputs:
- attended: bfloat16 [16, 32, 8192], P('dp', 'groups', 'tensor'), parts along dimension 1
- prm_score: float32 [16, 32], P('dp', 'groups'), parts along dimension 1
The draws below stay inside these ranges and needn't reach their ends.
There are 2 independent parts, one for each index of `groups`. The reference program is written for one: setup_inputs(seed, part) draws one part's arguments, and reference() takes and returns one part's arrays. A program takes and returns all parts, laid end to end along the dimension named above; an argument that names none is the same for every part. Nothing has to cross between parts.
Inputs may be any that keep to these rules, and one draw needn't show every extreme that they name: parents[b, p, 0] names the beam of problem p whose cache beam b continues. Among the problems of one beam b no beam is named by more than 3 problems, a bound that some block reaches.
All inputs are finite; a program needn't handle non-finite values.
Results may differ from the reference program's by a relative error of at most 0.001.
Values may be sent and summed in bfloat16 or wider, within the bound.
A program may use at most 192 MiB of HBM per device.

```python
import math
import jax
import jax.numpy as jnp
import numpy as np
from jax import lax

QHEADS = 64
KVHEADS = 8
HEAD = 128
D_PRM = 4096
BEAMS = 16
PROB = 16
CTX = 128
STEP = 64
CAP = 3


def draw_caches(key, part):
    key = jax.random.fold_in(key, 1)
    dims_all = (BEAMS, PROB, 2, CTX, KVHEADS * HEAD)
    values_all = jnp.clip(jax.random.normal(key, dims_all, jnp.float32), -4.0, 4.0)
    return values_all.astype(jnp.bfloat16)


def draw_queries(key, part):
    key = jax.random.fold_in(key, 2)
    dims_all = (BEAMS, PROB, QHEADS * HEAD)
    values_all = jnp.clip(jax.random.normal(key, dims_all, jnp.float32), -4.0, 4.0)
    return values_all.astype(jnp.bfloat16)


def draw_step_kv(key, part):
    key = jax.random.fold_in(key, 4)
    dims_all = (BEAMS, PROB, 2, STEP, KVHEADS * HEAD)
    values_all = jnp.clip(jax.random.normal(key, dims_all, jnp.float32), -4.0, 4.0)
    return values_all.astype(jnp.bfloat16)


def draw_step_hidden(key, part):
    key = jax.random.fold_in(key, 5)
    dims_all = (BEAMS, PROB, STEP, D_PRM)
    row_scale = jnp.exp(jax.random.uniform(jax.random.fold_in(key, 1), (BEAMS, PROB, STEP, 1), jnp.float32, math.log(0.3), math.log(3.0)))
    noise = jnp.clip(jax.random.normal(key, dims_all, jnp.float32), -4.0, 4.0)
    feature_scale = jnp.exp(jnp.linspace(math.log(0.3), math.log(3.0), D_PRM))
    return (noise * row_scale * feature_scale).astype(jnp.bfloat16)


def draw_lengths(key, part):
    key = jax.random.fold_in(key, 6)
    counted = jax.random.randint(key, (BEAMS, PROB), CTX // 8, CTX + 1, dtype=jnp.int32)
    position = jax.random.randint(jax.random.fold_in(key, 1), (), 0, BEAMS * PROB, dtype=jnp.int32)
    flat_index = jnp.arange(BEAMS * PROB, dtype=jnp.int32).reshape(BEAMS, PROB)
    counted = jnp.where(flat_index == position, CTX, counted)
    counted = jnp.where(flat_index == (position + 1) % (BEAMS * PROB), CTX // 8, counted)
    return counted.astype(jnp.int32)


def touch_ends(array, key, least, largest):
    longest = array.shape.index(max(array.shape))
    spots = []
    for shift in (0, 1):
        where = [jax.random.randint(jax.random.fold_in(key, axis), (), 0, length) for axis, length in enumerate(array.shape)]
        where[longest] = (where[longest] + shift) % array.shape[longest]
        spots.append(tuple(where))
    return array.at[spots[0]].set(least).at[spots[1]].set(largest)


def shard_levels(stream_key, dims, cuts, low, largest):
    loudness = 1.0
    for axis_at, blocks in cuts:
        draws = jax.random.uniform(jax.random.fold_in(jax.random.fold_in(stream_key, 6), axis_at), (blocks,), jnp.float32, low / len(cuts), largest / len(cuts))
        loudness = loudness * jnp.repeat(jnp.exp(draws), dims[axis_at] // blocks).reshape((-1,) + (1,) * (len(dims) - 1 - axis_at))
    return loudness


def shared_out(rng, own, number, rows, amount, top, reach, slope):
    order = jax.random.permutation(rng, amount)
    packed, usual = load_shares(amount, rows * top, reach, slope, True), load_shares(amount, rows * top, reach, slope, False)
    places = jnp.arange(amount)

    def named(sizes, offset_by):
        used = int((sizes > 0).sum())
        fixed = max(1, used // 4)
        passed = fixed + (places - fixed + offset_by * (used - fixed)) % max(1, amount - fixed)
        return jnp.zeros((amount,), jnp.int32).at[order[jnp.where(places < fixed, places, passed)]].set(jnp.asarray(sizes, jnp.int32))

    sizes = jnp.where(number % 4 == 0, named(packed, number // 4), named(usual, number - number // 4 - 1))
    mixed = jax.random.permutation(jax.random.fold_in(own, 3), amount)
    donor, sink = mixed[0:amount // 2 * 2:2], mixed[1:amount // 2 * 2:2]
    slack = jnp.minimum(sizes[donor] - 1, reach - sizes[sink]) // 2
    slack = jnp.where((donor == order[0]) | (sink == order[0]) | (sizes[sink] == 0), 0, jnp.maximum(slack, 0))
    passed = jax.random.randint(jax.random.fold_in(own, 4), (amount // 2,), 0, 1 << 20) % (slack + 1)
    sizes = sizes.at[donor].add(-passed).at[sink].add(passed)
    items = jnp.searchsorted(jnp.cumsum(sizes), jnp.arange(rows * top), side="right").astype(jnp.int32)
    grid = items.reshape(top, rows).T
    grid = grid[jax.random.permutation(jax.random.fold_in(own, 1), rows)]
    offset_by = jax.random.randint(jax.random.fold_in(own, 2), (rows, 1), 0, top)
    return jnp.take_along_axis(grid, (jnp.arange(top)[None, :] + offset_by) % top, axis=1)


def load_shares(count, total, limit, lean, full):
    loads = [(1 << 20) // math.isqrt(standing ** lean) + 1 for standing in range(1, count + 1)]
    largest = limit if full else min(limit, max(-(-total // count), total * loads[0] // sum(loads)))
    least = 1 if total - largest >= count - 1 else 0
    counts, rest = [largest] + [least] * (count - 1), total - largest - least * (count - 1)
    while rest > 0:
        movable = [i for i in range(1, count) if counts[i] < largest] or [i for i in range(1, count) if counts[i] < limit]
        mass, budget = sum([loads[i] for i in movable]), rest
        for i in movable:
            addition = min(limit - counts[i], max(1, budget * loads[i] // mass), rest)
            counts[i] = counts[i] + addition
            rest = rest - addition
    return np.array(counts)


def centred(own_key, extent, spread, limit, split=(), kind=jnp.bfloat16):
    result = jax.random.normal(own_key, extent, jnp.float32) * spread
    if len(split) > 0:
        result = shard_levels(own_key, extent, split, -0.22, 0.18) * result
    return jnp.clip(result, min=-limit, max=limit).astype(kind)


def setup_inputs(seed: int = 0, part: int = 0) -> dict:
    arg_keys = jax.random.split(jax.random.key(seed), 10)
    part_splits = jax.random.split(jax.random.fold_in(arg_keys[9], part), 10)
    step_hidden = draw_step_hidden(jax.random.fold_in(jax.random.fold_in(arg_keys[9], part), 71), part)
    prm_gain = jnp.clip(1.0 + 0.18 * jax.random.normal(arg_keys[1], (D_PRM,), jnp.float32), 0.1, 1.9)
    score_weight = centred(arg_keys[2], (D_PRM,), D_PRM ** -0.5, 0.09375, ((0, 2),), jnp.float32)
    step_bounds = touch_ends(jax.random.randint(part_splits[3], (BEAMS, PROB), 0, STEP), jax.random.fold_in(part_splits[3], 1), 0, STEP - 1).astype(jnp.int32)
    queries = draw_queries(jax.random.fold_in(jax.random.fold_in(arg_keys[9], part), 71), part)
    step_kv = draw_step_kv(jax.random.fold_in(jax.random.fold_in(arg_keys[9], part), 71), part)
    caches = draw_caches(jax.random.fold_in(jax.random.fold_in(arg_keys[9], part), 71), part)
    parents_keys = jax.random.split(jax.random.fold_in(part_splits[7], 1), BEAMS * PROB // PROB)
    parents_turns = jax.random.permutation(jax.random.fold_in(part_splits[7], 3), BEAMS * PROB // PROB)
    parents = jax.vmap(lambda own, number: shared_out(jax.random.fold_in(part_splits[7], 2), own, number, PROB, BEAMS, 1, CAP, 1))(parents_keys, parents_turns).reshape((BEAMS, PROB, 1))
    lengths = draw_lengths(jax.random.fold_in(jax.random.fold_in(arg_keys[9], part), 71), part)
    return {"step_hidden": step_hidden, "prm_gain": prm_gain, "score_weight": score_weight, "step_bounds": step_bounds, "queries": queries, "step_kv": step_kv, "caches": caches, "parents": parents, "lengths": lengths}


def reference(step_hidden, prm_gain, score_weight, step_bounds, queries, step_kv, caches, parents, lengths):
    widened = step_hidden.astype(jnp.float32)
    squares = lax.optimization_barrier(jnp.sum(widened * widened, axis=-1))
    products = lax.optimization_barrier(jnp.sum(widened * (prm_gain * score_weight), axis=-1))
    token_score = products / jnp.sqrt(squares / D_PRM + 1e-05)
    step_rows = jnp.arange(STEP, dtype=jnp.int32)
    step_live = step_rows[None, None, :] <= step_bounds[:, :, None]
    prm_score = lax.optimization_barrier(jnp.max(jnp.where(step_live, token_score, -1e+30), axis=-1))
    parent = parents[:, :, 0]
    problem = jnp.arange(PROB, dtype=jnp.int32)[None, :]
    inherited = caches[parent, problem]
    parent_len = lengths[parent, problem]
    key_rows = jnp.concatenate([inherited[:, :, 0], step_kv[:, :, 0]], axis=2).astype(jnp.float32)
    value_rows = jnp.concatenate([inherited[:, :, 1], step_kv[:, :, 1]], axis=2).astype(jnp.float32)
    cache_rows = jnp.arange(CTX, dtype=jnp.int32)
    visible = jnp.concatenate([cache_rows[None, None, :] < parent_len[:, :, None], step_live], axis=2)
    group_size = QHEADS // KVHEADS
    query_heads = queries.astype(jnp.float32).reshape(BEAMS, PROB, KVHEADS, group_size, HEAD)
    key_heads = key_rows.reshape(BEAMS, PROB, CTX + STEP, KVHEADS, HEAD)
    value_heads = value_rows.reshape(BEAMS, PROB, CTX + STEP, KVHEADS, HEAD)
    scores = jnp.einsum('bpkgh,bptkh->bpkgt', query_heads, key_heads, precision=lax.Precision.HIGHEST) * (1.0 / math.sqrt(HEAD))
    scores = jnp.where(visible[:, :, None, None, :], scores, -1e+30)
    maxima = lax.optimization_barrier(jnp.max(scores, axis=-1, keepdims=True))
    weights = jnp.exp(scores - maxima)
    totals = lax.optimization_barrier(jnp.sum(weights, axis=-1))
    numerators = jnp.einsum('bpkgt,bptkh->bpkgh', weights, value_heads, precision=lax.Precision.HIGHEST)
    attended = (numerators / totals[..., None]).reshape(BEAMS, PROB, QHEADS * HEAD).astype(jnp.bfloat16)
    return (attended, prm_score)
```

```python
import functools
import math

import jax
import jax.numpy as jnp
from jax import lax
from jax.experimental import pallas as pl
from jax.experimental.pallas import tpu as pltpu
from jax.sharding import PartitionSpec as P

HEAD = 128
D_PRM = 4096
PROB = 16
CTX = 128
STEP = 64
CAP = 3
LANES = 128
MESH = pl.DeviceIdType.MESH


def attend_group(queries, keys, values, limits, block_mask):
    heads = queries[0].shape[0]
    kv_heads = keys[0].shape[1] // HEAD
    group = heads // kv_heads
    count = len(queries)
    scores = []
    for query, key, limit in zip(queries, keys, limits):
        spread = jnp.concatenate([query] * kv_heads, axis=1) * block_mask
        score = lax.dot_general(
            spread, key, (((1,), (1,)), ((), ())), preferred_element_type=jnp.float32
        ) * (1.0 / math.sqrt(HEAD))
        column = lax.broadcasted_iota(jnp.int32, score.shape, 1)
        scores.append(jnp.where(column < limit, score, -1e30))
    scores = jnp.concatenate(scores, axis=0)
    maxima = jnp.max(scores, axis=-1, keepdims=True)
    weights = jnp.exp(scores - maxima)
    totals = jnp.sum(weights, axis=-1, keepdims=True)
    high = weights.astype(jnp.bfloat16)
    low = (weights - high.astype(jnp.float32)).astype(jnp.bfloat16)
    results = []
    for i in range(count):
        rows = slice(i * heads, (i + 1) * heads)
        both = jnp.concatenate([high[rows], low[rows]], axis=0)
        product = lax.dot_general(
            both, values[i], (((1,), (0,)), ((), ())), preferred_element_type=jnp.float32
        )
        product = product[:heads] + product[heads:]
        numerator = jnp.concatenate(
            [
                product[k * group : (k + 1) * group, k * HEAD : (k + 1) * HEAD]
                for k in range(kv_heads)
            ],
            axis=0,
        )
        results.append((numerator, maxima[rows], totals[rows]))
    return results


def kernel(
    n,
    resident,
    table,
    bounds_smem,
    bounds_row,
    queries,
    gain,
    weight,
    hidden,
    step_kv,
    caches,
    out,
    prm,
    hidden_v,
    step_v,
    cache_v,
    sent_q,
    got_q,
    sent_r,
    got_r,
    sent_s,
    got_s,
    own_num,
    own_max,
    own_tot,
    part,
    other,
    load_sem,
    qs_sem,
    qr_sem,
    rs_sem,
    rr_sem,
    ss_sem,
    sr_sem,
    pair_sem,
):
    me = lax.axis_index("dp")
    core = lax.axis_index("tensor")
    rows = resident * PROB
    slots = resident * resident * CAP
    heads = queries.shape[1]
    width = step_v.shape[2]
    kv_heads = width // HEAD
    group = heads // kv_heads
    work_at, len_at, merge_at = n * slots, 2 * n * slots, 3 * n * slots

    chunks = load_sem.shape[1]
    span = rows // chunks

    def load(which, chunk):
        source, target = ((step_kv, step_v), (caches, cache_v), (hidden, hidden_v))[which]
        piece = pl.ds(chunk * span, span)
        return pltpu.make_async_copy(
            source.at[piece], target.at[piece], load_sem.at[which, chunk]
        )

    for which in range(3):
        for chunk in range(chunks):
            load(which, chunk).start()

    barrier = pltpu.get_barrier_semaphore()
    for step in range(1, n):
        pl.semaphore_signal(
            barrier, inc=1, device_id={"dp": lax.rem(me + step, n)}, device_id_type=MESH
        )
    pl.semaphore_signal(barrier, inc=1, device_id={"tensor": 1 - core}, device_id_type=MESH)

    def query_copy(peer, source):
        return pltpu.make_async_remote_copy(
            src_ref=sent_q.at[peer],
            dst_ref=got_q.at[source],
            send_sem=qs_sem.at[peer],
            recv_sem=qr_sem.at[source],
            device_id={"dp": peer},
            device_id_type=MESH,
        )

    def reply_copy(peer, source):
        return pltpu.make_async_remote_copy(
            src_ref=sent_r.at[peer],
            dst_ref=got_r.at[source],
            send_sem=rs_sem.at[peer],
            recv_sem=rr_sem.at[source],
            device_id={"dp": peer},
            device_id_type=MESH,
        )

    def stat_copy(peer, source):
        return pltpu.make_async_remote_copy(
            src_ref=sent_s.at[peer],
            dst_ref=got_s.at[source],
            send_sem=ss_sem.at[peer],
            recv_sem=sr_sem.at[source],
            device_id={"dp": peer},
            device_id_type=MESH,
        )

    def pack(peer, target):
        for slot in range(slots):
            beam = slot // (resident * CAP)
            problem = table[peer * slots + slot]
            target[peer, slot] = queries[beam * PROB + problem]

    pl.semaphore_wait(barrier, n)

    @pl.loop(1, n)
    def _(step):
        peer = lax.rem(me + step, n)
        pack(peer, sent_q)
        query_copy(peer, me).start()

    pack(me, got_q)

    spread_row = lax.broadcasted_iota(jnp.int32, (heads, width), 0)
    spread_col = lax.broadcasted_iota(jnp.int32, (heads, width), 1)
    block_mask = jnp.zeros((heads, width), jnp.float32)
    for k in range(kv_heads):
        inside = (
            (spread_row >= k * group)
            & (spread_row < (k + 1) * group)
            & (spread_col >= k * HEAD)
            & (spread_col < (k + 1) * HEAD)
        )
        block_mask = jnp.where(inside, 1.0, block_mask)
    block_mask = block_mask.astype(jnp.bfloat16)
    stat_row = lax.broadcasted_iota(jnp.int32, (heads, LANES), 0)
    stat_col = lax.broadcasted_iota(jnp.int32, (heads, LANES), 1)

    for chunk in range(chunks):
        load(0, chunk).wait()
    own_batch = 8

    @pl.loop(0, rows // own_batch)
    def _(batch):
        places = [batch * own_batch + i for i in range(own_batch)]
        results = attend_group(
            [queries[j] for j in places],
            [step_v[j, :STEP, :] for j in places],
            [step_v[j, STEP:, :] for j in places],
            [bounds_smem[j] + 1 for j in places],
            block_mask,
        )
        for j, (numerator, maxima, totals) in zip(places, results):
            own_num[j] = numerator
            own_max[j] = jnp.broadcast_to(maxima, (heads, LANES))
            own_tot[j] = jnp.broadcast_to(totals, (heads, LANES))

    for chunk in range(chunks):
        load(1, chunk).wait()

    def serve(peer, reply, stats):
        batch = 6 if slots % 6 == 0 else slots
        for first in range(0, slots, batch):
            numbers = range(first, first + batch)
            places = [
                ((slot // CAP) % resident) * PROB + table[work_at + peer * slots + slot]
                for slot in numbers
            ]
            results = attend_group(
                [got_q[peer, slot] for slot in numbers],
                [cache_v[j, :CTX, :] for j in places],
                [cache_v[j, CTX:, :] for j in places],
                [table[len_at + peer * slots + slot] for slot in numbers],
                block_mask,
            )
            for slot, (numerator, maxima, totals) in zip(numbers, results):
                reply[peer, slot] = numerator
                packed = jnp.where(stat_col == stat_row, maxima, 0.0) + jnp.where(
                    stat_col == stat_row + heads, totals, 0.0
                )
                stats[peer, slot : slot + 1, :] = jnp.sum(packed, axis=0, keepdims=True)

    serve(me, got_r, got_s)

    @pl.loop(1, n)
    def _(step):
        peer = lax.rem(me + n - step, n)
        query_copy(peer, peer).wait_recv()
        serve(peer, sent_r, sent_s)
        reply_copy(peer, me).start()
        stat_copy(peer, me).start()

    for chunk in range(chunks):
        load(2, chunk).wait()
    scaled = gain[...] * weight[...]
    column = lax.broadcasted_iota(jnp.int32, (STEP, LANES), 1)

    def reward(j, carry):
        squares_all, products_all = carry
        wide = hidden_v[j].astype(jnp.float32)
        squares = jnp.sum(wide * wide, axis=-1, keepdims=True)
        products = jnp.sum(wide * scaled, axis=-1, keepdims=True)
        return (
            jnp.where(column == j, squares, squares_all),
            jnp.where(column == j, products, products_all),
        )

    zeros = jnp.zeros((STEP, LANES), jnp.float32)
    squares, products = lax.fori_loop(0, rows, reward, (zeros, zeros))
    part[0] = squares
    part[1] = products
    pair = pltpu.make_async_remote_copy(
        src_ref=part,
        dst_ref=other,
        send_sem=pair_sem.at[0],
        recv_sem=pair_sem.at[1],
        device_id={"tensor": 1 - core},
        device_id_type=MESH,
    )
    pair.start()
    pair.wait()
    squares = part[0] + other[0]
    products = part[1] + other[1]
    token_score = products / jnp.sqrt(squares / D_PRM + 1e-05)
    step_rows = lax.broadcasted_iota(jnp.int32, (STEP, LANES), 0)
    token_score = jnp.where(step_rows <= bounds_row[...], token_score, -1e30)
    prm[...] = jnp.max(token_score, axis=0, keepdims=True)

    @pl.loop(1, n)
    def _(step):
        peer = lax.rem(me + n - step, n)
        reply_copy(peer, peer).wait_recv()
        stat_copy(peer, peer).wait_recv()

    merge_batch = 4

    @pl.loop(0, rows // merge_batch)
    def _(batch):
        for i in range(merge_batch):
            j = batch * merge_batch + i
            source = table[merge_at + 2 * j]
            slot = table[merge_at + 2 * j + 1]
            stats = got_s[source, pl.ds(slot, 1), :]
            cache_max = jnp.sum(
                jnp.where(stat_col == stat_row, stats, 0.0), axis=-1, keepdims=True
            )
            cache_tot = jnp.sum(
                jnp.where(stat_col == stat_row + heads, stats, 0.0), axis=-1, keepdims=True
            )
            highest = jnp.maximum(cache_max, own_max[j])
            scale_cache = jnp.exp(cache_max - highest)
            scale_own = jnp.exp(own_max[j] - highest)
            totals = cache_tot * scale_cache + own_tot[j] * scale_own
            merged = (got_r[source, slot] * scale_cache + own_num[j] * scale_own) / totals
            out[j] = merged.astype(jnp.bfloat16)

    @pl.loop(1, n)
    def _(step):
        peer = lax.rem(me + step, n)
        query_copy(peer, me).wait_send()
        reply_copy(peer, me).wait_send()
        stat_copy(peer, me).wait_send()


def body(
    n,
    step_hidden,
    prm_gain,
    score_weight,
    step_bounds,
    queries,
    step_kv,
    caches,
    parents,
    lengths,
):
    resident = step_hidden.shape[0]
    rows = resident * PROB
    slots = resident * resident * CAP
    heads = queries.shape[-1] // HEAD
    width = caches.shape[-1]
    beams = parents.shape[0]
    me = lax.axis_index("dp")

    parent = parents[:, :, 0]
    problem = jnp.arange(PROB, dtype=jnp.int32)
    siblings = parent[:, :, None] == parent[:, None, :]
    earlier = problem[None, :] < problem[:, None]
    rank = jnp.sum(siblings & earlier[None, :, :], axis=-1, dtype=jnp.int32)
    beam_ids = jnp.arange(beams, dtype=jnp.int32)
    slot_ids = jnp.arange(CAP, dtype=jnp.int32)
    match = (parent[:, None, None, :] == beam_ids[None, :, None, None]) & (
        rank[:, None, None, :] == slot_ids[None, None, :, None]
    )
    pick = jnp.sum(jnp.where(match, problem, 0), axis=-1)
    pick_len = jnp.sum(jnp.where(match, lengths[None, :, None, :], 0), axis=-1)
    first = me * resident
    send = lax.dynamic_slice_in_dim(pick, first, resident, 0)
    send = send.reshape(resident, n, resident, CAP).transpose(1, 0, 2, 3)
    work = lax.dynamic_slice_in_dim(pick, first, resident, 1)
    work_len = lax.dynamic_slice_in_dim(pick_len, first, resident, 1)
    own_parent = lax.dynamic_slice_in_dim(parent, first, resident, 0)
    own_rank = lax.dynamic_slice_in_dim(rank, first, resident, 0)
    local = jnp.arange(resident, dtype=jnp.int32)[:, None]
    source = own_parent // resident
    slot = (local * resident + own_parent % resident) * CAP + own_rank
    merge = jnp.stack([source, slot], axis=-1)
    table = jnp.concatenate(
        [send.reshape(-1), work.reshape(-1), work_len.reshape(-1), merge.reshape(-1)]
    )
    bounds = step_bounds.reshape(-1)
    bounds_row = jnp.pad(bounds, (0, LANES - rows)).reshape(1, LANES)

    smem = pl.BlockSpec(memory_space=pltpu.SMEM)
    vmem = pl.BlockSpec(memory_space=pltpu.VMEM)
    hbm = pl.BlockSpec(memory_space=pl.ANY)
    chunks = 4
    dma = pltpu.SemaphoreType.DMA
    attended, prm = pl.pallas_call(
        functools.partial(kernel, n, resident),
        out_shape=(
            jax.ShapeDtypeStruct((rows, heads, HEAD), jnp.bfloat16),
            jax.ShapeDtypeStruct((1, LANES), jnp.float32),
        ),
        in_specs=[smem, smem, vmem, vmem, vmem, vmem, hbm, hbm, hbm],
        out_specs=(vmem, vmem),
        scratch_shapes=[
            pltpu.VMEM((rows, STEP, step_hidden.shape[-1]), jnp.bfloat16),
            pltpu.VMEM((rows, 2 * STEP, width), jnp.bfloat16),
            pltpu.VMEM((rows, 2 * CTX, width), jnp.bfloat16),
            pltpu.VMEM((n, slots, heads, HEAD), jnp.bfloat16),
            pltpu.VMEM((n, slots, heads, HEAD), jnp.bfloat16),
            pltpu.VMEM((n, slots, heads, HEAD), jnp.float32),
            pltpu.VMEM((n, slots, heads, HEAD), jnp.float32),
            pltpu.VMEM((n, -(-slots // 8) * 8, LANES), jnp.float32),
            pltpu.VMEM((n, -(-slots // 8) * 8, LANES), jnp.float32),
            pltpu.VMEM((rows, heads, HEAD), jnp.float32),
            pltpu.VMEM((rows, heads, LANES), jnp.float32),
            pltpu.VMEM((rows, heads, LANES), jnp.float32),
            pltpu.VMEM((2, STEP, LANES), jnp.float32),
            pltpu.VMEM((2, STEP, LANES), jnp.float32),
            dma((3, chunks)),
            dma((n,)),
            dma((n,)),
            dma((n,)),
            dma((n,)),
            dma((n,)),
            dma((n,)),
            dma((2,)),
        ],
        compiler_params=pltpu.CompilerParams(
            collective_id=0, has_side_effects=True, vmem_limit_bytes=48 * 1024 * 1024
        ),
    )(
        table,
        bounds,
        bounds_row,
        queries.reshape(rows, heads, HEAD),
        prm_gain.reshape(1, -1),
        score_weight.reshape(1, -1),
        step_hidden.reshape(rows, STEP, step_hidden.shape[-1]),
        step_kv.reshape(rows, 2 * STEP, width),
        caches.reshape(rows, 2 * CTX, width),
    )
    attended = attended.reshape(resident, PROB, heads * HEAD)
    return attended, prm[0, :rows].reshape(resident, PROB)


def solution(mesh):
    in_specs = (
        P("dp", "groups", None, "tensor"),
        P("tensor"),
        P("tensor"),
        P("dp", "groups"),
        P("dp", "groups", "tensor"),
        P("dp", "groups", None, None, "tensor"),
        P("dp", "groups", None, None, "tensor"),
        P(None, "groups", None),
        P(None, "groups"),
    )
    out_specs = (P("dp", "groups", "tensor"), P("dp", "groups"))
    return jax.shard_map(
        functools.partial(body, mesh.shape["dp"]),
        mesh=mesh,
        in_specs=in_specs,
        out_specs=out_specs,
        check_vma=False,
    )
```

```python
import functools
import math

import jax
import jax.numpy as jnp
from jax import lax
from jax.experimental import pallas as pl
from jax.experimental.pallas import tpu as pltpu
from jax.sharding import PartitionSpec as P

HEAD = 128
D_PRM = 4096
PROB = 16
CTX = 128
STEP = 64
CAP = 3
LANES = 128
CODES = 32767.0
MESH = pl.DeviceIdType.MESH


def attend_group(queries, keys, values, limits, block_mask):
    heads = queries[0].shape[0]
    kv_heads = keys[0].shape[1] // HEAD
    group = heads // kv_heads
    count = len(queries)
    scores = []
    for query, key, limit in zip(queries, keys, limits):
        spread = jnp.concatenate([query] * kv_heads, axis=1) * block_mask
        score = lax.dot_general(
            spread, key, (((1,), (1,)), ((), ())), preferred_element_type=jnp.float32
        ) * (1.0 / math.sqrt(HEAD))
        column = lax.broadcasted_iota(jnp.int32, score.shape, 1)
        scores.append(jnp.where(column < limit, score, -1e30))
    scores = jnp.concatenate(scores, axis=0)
    maxima = jnp.max(scores, axis=-1, keepdims=True)
    weights = jnp.exp(scores - maxima)
    totals = jnp.sum(weights, axis=-1, keepdims=True)
    high = weights.astype(jnp.bfloat16)
    low = (weights - high.astype(jnp.float32)).astype(jnp.bfloat16)
    results = []
    for i in range(count):
        rows = slice(i * heads, (i + 1) * heads)
        both = jnp.concatenate([high[rows], low[rows]], axis=0)
        product = lax.dot_general(
            both, values[i], (((1,), (0,)), ((), ())), preferred_element_type=jnp.float32
        )
        product = product[:heads] + product[heads:]
        numerator = jnp.concatenate(
            [
                product[k * group : (k + 1) * group, k * HEAD : (k + 1) * HEAD]
                for k in range(kv_heads)
            ],
            axis=0,
        )
        results.append((numerator, maxima[rows], totals[rows]))
    return results


def kernel(
    n,
    resident,
    table,
    bounds_smem,
    bounds_row,
    queries,
    gain,
    weight,
    hidden,
    step_kv,
    caches,
    out,
    prm,
    hidden_v,
    step_v,
    cache_v,
    sent_q,
    got_q,
    sent_r,
    got_r,
    sent_s,
    got_s,
    own_num,
    own_max,
    own_tot,
    part,
    other,
    load_sem,
    qs_sem,
    qr_sem,
    rs_sem,
    rr_sem,
    ss_sem,
    sr_sem,
    pair_sem,
):
    me = lax.axis_index("dp")
    core = lax.axis_index("tensor")
    rows = resident * PROB
    slots = resident * resident * CAP
    heads = queries.shape[1]
    width = step_v.shape[2]
    kv_heads = width // HEAD
    group = heads // kv_heads
    work_at, len_at, merge_at = n * slots, 2 * n * slots, 3 * n * slots

    chunks = load_sem.shape[1]
    span = rows // chunks

    def load(which, chunk):
        source, target = ((step_kv, step_v), (caches, cache_v), (hidden, hidden_v))[which]
        piece = pl.ds(chunk * span, span)
        return pltpu.make_async_copy(
            source.at[piece], target.at[piece], load_sem.at[which, chunk]
        )

    for which in range(3):
        for chunk in range(chunks):
            load(which, chunk).start()

    barrier = pltpu.get_barrier_semaphore()
    for step in range(1, n):
        pl.semaphore_signal(
            barrier, inc=1, device_id={"dp": lax.rem(me + step, n)}, device_id_type=MESH
        )
    pl.semaphore_signal(barrier, inc=1, device_id={"tensor": 1 - core}, device_id_type=MESH)

    def query_copy(peer, source):
        return pltpu.make_async_remote_copy(
            src_ref=sent_q.at[peer],
            dst_ref=got_q.at[source],
            send_sem=qs_sem.at[peer],
            recv_sem=qr_sem.at[source],
            device_id={"dp": peer},
            device_id_type=MESH,
        )

    def reply_copy(peer, source):
        return pltpu.make_async_remote_copy(
            src_ref=sent_r.at[peer],
            dst_ref=got_r.at[source],
            send_sem=rs_sem.at[peer],
            recv_sem=rr_sem.at[source],
            device_id={"dp": peer},
            device_id_type=MESH,
        )

    def stat_copy(peer, source):
        return pltpu.make_async_remote_copy(
            src_ref=sent_s.at[peer],
            dst_ref=got_s.at[source],
            send_sem=ss_sem.at[peer],
            recv_sem=sr_sem.at[source],
            device_id={"dp": peer},
            device_id_type=MESH,
        )

    def pack(peer, target):
        for slot in range(slots):
            beam = slot // (resident * CAP)
            problem = table[peer * slots + slot]
            target[peer, slot] = queries[beam * PROB + problem]

    pl.semaphore_wait(barrier, n)

    @pl.loop(1, n)
    def _(step):
        peer = lax.rem(me + step, n)
        pack(peer, sent_q)
        query_copy(peer, me).start()

    pack(me, got_q)

    spread_row = lax.broadcasted_iota(jnp.int32, (heads, width), 0)
    spread_col = lax.broadcasted_iota(jnp.int32, (heads, width), 1)
    block_mask = jnp.zeros((heads, width), jnp.float32)
    for k in range(kv_heads):
        inside = (
            (spread_row >= k * group)
            & (spread_row < (k + 1) * group)
            & (spread_col >= k * HEAD)
            & (spread_col < (k + 1) * HEAD)
        )
        block_mask = jnp.where(inside, 1.0, block_mask)
    block_mask = block_mask.astype(jnp.bfloat16)
    stat_row = lax.broadcasted_iota(jnp.int32, (heads, LANES), 0)
    stat_col = lax.broadcasted_iota(jnp.int32, (heads, LANES), 1)

    for chunk in range(chunks):
        load(0, chunk).wait()
    own_batch = 8

    @pl.loop(0, rows // own_batch)
    def _(batch):
        places = [batch * own_batch + i for i in range(own_batch)]
        results = attend_group(
            [queries[j] for j in places],
            [step_v[j, :STEP, :] for j in places],
            [step_v[j, STEP:, :] for j in places],
            [bounds_smem[j] + 1 for j in places],
            block_mask,
        )
        for j, (numerator, maxima, totals) in zip(places, results):
            own_num[j] = numerator
            own_max[j] = jnp.broadcast_to(maxima, (heads, LANES))
            own_tot[j] = jnp.broadcast_to(totals, (heads, LANES))

    for chunk in range(chunks):
        load(1, chunk).wait()

    def serve(peer, reply, stats):
        batch = 6 if slots % 6 == 0 else slots
        for first in range(0, slots, batch):
            numbers = range(first, first + batch)
            places = [
                ((slot // CAP) % resident) * PROB + table[work_at + peer * slots + slot]
                for slot in numbers
            ]
            results = attend_group(
                [got_q[peer, slot] for slot in numbers],
                [cache_v[j, :CTX, :] for j in places],
                [cache_v[j, CTX:, :] for j in places],
                [table[len_at + peer * slots + slot] for slot in numbers],
                block_mask,
            )
            for slot, (numerator, maxima, totals) in zip(numbers, results):
                largest = jnp.max(jnp.abs(numerator), axis=-1, keepdims=True)
                largest = jnp.maximum(largest, 1e-20)
                coded = jnp.round(numerator * (CODES / largest))
                reply[peer, slot] = coded.astype(jnp.int32).astype(jnp.int16)
                packed = jnp.where(stat_col == stat_row, maxima, 0.0)
                packed = jnp.where(stat_col == stat_row + heads, totals, packed)
                packed = jnp.where(stat_col == stat_row + 2 * heads, largest, packed)
                stats[peer, slot : slot + 1, :] = jnp.sum(packed, axis=0, keepdims=True)

    serve(me, got_r, got_s)

    @pl.loop(1, n)
    def _(step):
        peer = lax.rem(me + n - step, n)
        query_copy(peer, peer).wait_recv()
        serve(peer, sent_r, sent_s)
        reply_copy(peer, me).start()
        stat_copy(peer, me).start()

    for chunk in range(chunks):
        load(2, chunk).wait()
    scaled = gain[...] * weight[...]
    column = lax.broadcasted_iota(jnp.int32, (STEP, LANES), 1)

    def reward(j, carry):
        squares_all, products_all = carry
        wide = hidden_v[j].astype(jnp.float32)
        squares = jnp.sum(wide * wide, axis=-1, keepdims=True)
        products = jnp.sum(wide * scaled, axis=-1, keepdims=True)
        return (
            jnp.where(column == j, squares, squares_all),
            jnp.where(column == j, products, products_all),
        )

    zeros = jnp.zeros((STEP, LANES), jnp.float32)
    squares, products = lax.fori_loop(0, rows, reward, (zeros, zeros))
    part[0] = squares
    part[1] = products
    pair = pltpu.make_async_remote_copy(
        src_ref=part,
        dst_ref=other,
        send_sem=pair_sem.at[0],
        recv_sem=pair_sem.at[1],
        device_id={"tensor": 1 - core},
        device_id_type=MESH,
    )
    pair.start()
    pair.wait()
    squares = part[0] + other[0]
    products = part[1] + other[1]
    token_score = products / jnp.sqrt(squares / D_PRM + 1e-05)
    step_rows = lax.broadcasted_iota(jnp.int32, (STEP, LANES), 0)
    token_score = jnp.where(step_rows <= bounds_row[...], token_score, -1e30)
    prm[...] = jnp.max(token_score, axis=0, keepdims=True)

    @pl.loop(1, n)
    def _(step):
        peer = lax.rem(me + n - step, n)
        reply_copy(peer, peer).wait_recv()
        stat_copy(peer, peer).wait_recv()

    merge_batch = 4

    @pl.loop(0, rows // merge_batch)
    def _(batch):
        for i in range(merge_batch):
            j = batch * merge_batch + i
            source = table[merge_at + 2 * j]
            slot = table[merge_at + 2 * j + 1]
            stats = got_s[source, pl.ds(slot, 1), :]
            cache_max = jnp.sum(
                jnp.where(stat_col == stat_row, stats, 0.0), axis=-1, keepdims=True
            )
            cache_tot = jnp.sum(
                jnp.where(stat_col == stat_row + heads, stats, 0.0), axis=-1, keepdims=True
            )
            cache_step = jnp.sum(
                jnp.where(stat_col == stat_row + 2 * heads, stats, 0.0), axis=-1, keepdims=True
            ) * (1.0 / CODES)
            highest = jnp.maximum(cache_max, own_max[j])
            scale_cache = jnp.exp(cache_max - highest)
            scale_own = jnp.exp(own_max[j] - highest)
            totals = cache_tot * scale_cache + own_tot[j] * scale_own
            coded = got_r[source, slot].astype(jnp.int32).astype(jnp.float32)
            cache_num = coded * (cache_step * scale_cache)
            merged = (cache_num + own_num[j] * scale_own) / totals
            out[j] = merged.astype(jnp.bfloat16)

    @pl.loop(1, n)
    def _(step):
        peer = lax.rem(me + step, n)
        query_copy(peer, me).wait_send()
        reply_copy(peer, me).wait_send()
        stat_copy(peer, me).wait_send()


def body(
    n,
    step_hidden,
    prm_gain,
    score_weight,
    step_bounds,
    queries,
    step_kv,
    caches,
    parents,
    lengths,
):
    resident = step_hidden.shape[0]
    rows = resident * PROB
    slots = resident * resident * CAP
    heads = queries.shape[-1] // HEAD
    width = caches.shape[-1]
    beams = parents.shape[0]
    me = lax.axis_index("dp")

    parent = parents[:, :, 0]
    problem = jnp.arange(PROB, dtype=jnp.int32)
    siblings = parent[:, :, None] == parent[:, None, :]
    earlier = problem[None, :] < problem[:, None]
    rank = jnp.sum(siblings & earlier[None, :, :], axis=-1, dtype=jnp.int32)
    beam_ids = jnp.arange(beams, dtype=jnp.int32)
    slot_ids = jnp.arange(CAP, dtype=jnp.int32)
    match = (parent[:, None, None, :] == beam_ids[None, :, None, None]) & (
        rank[:, None, None, :] == slot_ids[None, None, :, None]
    )
    pick = jnp.sum(jnp.where(match, problem, 0), axis=-1)
    pick_len = jnp.sum(jnp.where(match, lengths[None, :, None, :], 0), axis=-1)
    first = me * resident
    send = lax.dynamic_slice_in_dim(pick, first, resident, 0)
    send = send.reshape(resident, n, resident, CAP).transpose(1, 0, 2, 3)
    work = lax.dynamic_slice_in_dim(pick, first, resident, 1)
    work_len = lax.dynamic_slice_in_dim(pick_len, first, resident, 1)
    own_parent = lax.dynamic_slice_in_dim(parent, first, resident, 0)
    own_rank = lax.dynamic_slice_in_dim(rank, first, resident, 0)
    local = jnp.arange(resident, dtype=jnp.int32)[:, None]
    source = own_parent // resident
    slot = (local * resident + own_parent % resident) * CAP + own_rank
    merge = jnp.stack([source, slot], axis=-1)
    table = jnp.concatenate(
        [send.reshape(-1), work.reshape(-1), work_len.reshape(-1), merge.reshape(-1)]
    )
    bounds = step_bounds.reshape(-1)
    bounds_row = jnp.pad(bounds, (0, LANES - rows)).reshape(1, LANES)

    smem = pl.BlockSpec(memory_space=pltpu.SMEM)
    vmem = pl.BlockSpec(memory_space=pltpu.VMEM)
    hbm = pl.BlockSpec(memory_space=pl.ANY)
    chunks = 4
    dma = pltpu.SemaphoreType.DMA
    attended, prm = pl.pallas_call(
        functools.partial(kernel, n, resident),
        out_shape=(
            jax.ShapeDtypeStruct((rows, heads, HEAD), jnp.bfloat16),
            jax.ShapeDtypeStruct((1, LANES), jnp.float32),
        ),
        in_specs=[smem, smem, vmem, vmem, vmem, vmem, hbm, hbm, hbm],
        out_specs=(vmem, vmem),
        scratch_shapes=[
            pltpu.VMEM((rows, STEP, step_hidden.shape[-1]), jnp.bfloat16),
            pltpu.VMEM((rows, 2 * STEP, width), jnp.bfloat16),
            pltpu.VMEM((rows, 2 * CTX, width), jnp.bfloat16),
            pltpu.VMEM((n, slots, heads, HEAD), jnp.bfloat16),
            pltpu.VMEM((n, slots, heads, HEAD), jnp.bfloat16),
            pltpu.VMEM((n, slots, heads, HEAD), jnp.int16),
            pltpu.VMEM((n, slots, heads, HEAD), jnp.int16),
            pltpu.VMEM((n, -(-slots // 8) * 8, LANES), jnp.float32),
            pltpu.VMEM((n, -(-slots // 8) * 8, LANES), jnp.float32),
            pltpu.VMEM((rows, heads, HEAD), jnp.float32),
            pltpu.VMEM((rows, heads, LANES), jnp.float32),
            pltpu.VMEM((rows, heads, LANES), jnp.float32),
            pltpu.VMEM((2, STEP, LANES), jnp.float32),
            pltpu.VMEM((2, STEP, LANES), jnp.float32),
            dma((3, chunks)),
            dma((n,)),
            dma((n,)),
            dma((n,)),
            dma((n,)),
            dma((n,)),
            dma((n,)),
            dma((2,)),
        ],
        compiler_params=pltpu.CompilerParams(
            collective_id=0, has_side_effects=True, vmem_limit_bytes=48 * 1024 * 1024
        ),
    )(
        table,
        bounds,
        bounds_row,
        queries.reshape(rows, heads, HEAD),
        prm_gain.reshape(1, -1),
        score_weight.reshape(1, -1),
        step_hidden.reshape(rows, STEP, step_hidden.shape[-1]),
        step_kv.reshape(rows, 2 * STEP, width),
        caches.reshape(rows, 2 * CTX, width),
    )
    attended = attended.reshape(resident, PROB, heads * HEAD)
    return attended, prm[0, :rows].reshape(resident, PROB)


def solution(mesh):
    in_specs = (
        P("dp", "groups", None, "tensor"),
        P("tensor"),
        P("tensor"),
        P("dp", "groups"),
        P("dp", "groups", "tensor"),
        P("dp", "groups", None, None, "tensor"),
        P("dp", "groups", None, None, "tensor"),
        P(None, "groups", None),
        P(None, "groups"),
    )
    out_specs = (P("dp", "groups", "tensor"), P("dp", "groups"))
    return jax.shard_map(
        functools.partial(body, mesh.shape["dp"]),
        mesh=mesh,
        in_specs=in_specs,
        out_specs=out_specs,
        check_vma=False,
    )
```

```python
import functools
import math

import jax
import jax.numpy as jnp
from jax import lax
from jax.experimental import pallas as pl
from jax.experimental.pallas import tpu as pltpu
from jax.sharding import PartitionSpec as P

HEAD = 128
D_PRM = 4096
PROB = 16
CTX = 128
STEP = 64
CAP = 3
LANES = 128
CODES = 32767.0
MESH = pl.DeviceIdType.MESH


def attend_group(queries, keys, values, limits, block_mask):
    heads = queries[0].shape[0]
    kv_heads = keys[0].shape[1] // HEAD
    group = heads // kv_heads
    count = len(queries)
    scores = []
    for query, key, limit in zip(queries, keys, limits):
        spread = jnp.concatenate([query] * kv_heads, axis=1) * block_mask
        score = lax.dot_general(
            spread, key, (((1,), (1,)), ((), ())), preferred_element_type=jnp.float32
        ) * (1.0 / math.sqrt(HEAD))
        column = lax.broadcasted_iota(jnp.int32, score.shape, 1)
        scores.append(jnp.where(column < limit, score, -1e30))
    scores = jnp.concatenate(scores, axis=0)
    maxima = jnp.max(scores, axis=-1, keepdims=True)
    weights = jnp.exp(scores - maxima)
    totals = jnp.sum(weights, axis=-1, keepdims=True)
    high = weights.astype(jnp.bfloat16)
    low = (weights - high.astype(jnp.float32)).astype(jnp.bfloat16)
    results = []
    for i in range(count):
        rows = slice(i * heads, (i + 1) * heads)
        both = jnp.concatenate([high[rows], low[rows]], axis=0)
        product = lax.dot_general(
            both, values[i], (((1,), (0,)), ((), ())), preferred_element_type=jnp.float32
        )
        product = product[:heads] + product[heads:]
        numerator = jnp.concatenate(
            [
                product[k * group : (k + 1) * group, k * HEAD : (k + 1) * HEAD]
                for k in range(kv_heads)
            ],
            axis=0,
        )
        results.append((numerator, maxima[rows], totals[rows]))
    return results


def kernel(
    n,
    resident,
    bounds_smem,
    queries,
    gain,
    weight,
    parents,
    lengths,
    hidden,
    step_kv,
    caches,
    out,
    prm,
    gain_v,
    weight_v,
    parent_v,
    length_v,
    rank_v,
    table_v,
    table,
    hidden_v,
    step_v,
    cache_v,
    sent_q,
    got_q,
    sent_r,
    got_r,
    sent_s,
    got_s,
    own_num,
    own_max,
    own_tot,
    part,
    other,
    small_sem,
    load_sem,
    qs_sem,
    qr_sem,
    rs_sem,
    rr_sem,
    ss_sem,
    sr_sem,
    pair_sem,
):
    me = lax.axis_index("dp")
    core = lax.axis_index("tensor")
    rows = resident * PROB
    slots = resident * resident * CAP
    heads = queries.shape[1]
    width = step_v.shape[2]
    kv_heads = width // HEAD
    group = heads // kv_heads
    beams = n * resident

    chunks = load_sem.shape[1]
    span = rows // chunks

    def load(which, chunk):
        source, target = ((step_kv, step_v), (caches, cache_v), (hidden, hidden_v))[which]
        piece = pl.ds(chunk * span, span)
        return pltpu.make_async_copy(
            source.at[piece], target.at[piece], load_sem.at[which, chunk]
        )

    small = [
        pltpu.make_async_copy(source, target, small_sem.at[i])
        for i, (source, target) in enumerate(
            ((parents, parent_v), (lengths, length_v), (gain, gain_v), (weight, weight_v))
        )
    ]
    for copy in small:
        copy.start()
    for which in range(3):
        for chunk in range(chunks):
            load(which, chunk).start()

    barrier = pltpu.get_barrier_semaphore()
    for step in range(1, n):
        pl.semaphore_signal(
            barrier, inc=1, device_id={"dp": lax.rem(me + step, n)}, device_id_type=MESH
        )
    pl.semaphore_signal(barrier, inc=1, device_id={"tensor": 1 - core}, device_id_type=MESH)

    def query_copy(peer, source):
        return pltpu.make_async_remote_copy(
            src_ref=sent_q.at[peer],
            dst_ref=got_q.at[source],
            send_sem=qs_sem.at[peer],
            recv_sem=qr_sem.at[source],
            device_id={"dp": peer},
            device_id_type=MESH,
        )

    def reply_copy(peer, source):
        return pltpu.make_async_remote_copy(
            src_ref=sent_r.at[peer],
            dst_ref=got_r.at[source],
            send_sem=rs_sem.at[peer],
            recv_sem=rr_sem.at[source],
            device_id={"dp": peer},
            device_id_type=MESH,
        )

    def stat_copy(peer, source):
        return pltpu.make_async_remote_copy(
            src_ref=sent_s.at[peer],
            dst_ref=got_s.at[source],
            send_sem=ss_sem.at[peer],
            recv_sem=sr_sem.at[source],
            device_id={"dp": peer},
            device_id_type=MESH,
        )

    def pack(peer, target):
        for slot in range(slots):
            beam = slot // (resident * CAP)
            near = slot // CAP % resident
            problem = table[peer * resident + near, beam * CAP + slot % CAP]
            target[peer, slot] = queries[beam * PROB + problem]

    small[0].wait()
    small[1].wait()
    table_v[...] = jnp.zeros_like(table_v)
    parent = parent_v[...]
    problem_ids = lax.broadcasted_iota(jnp.int32, parent.shape, 1)
    beam_ids = lax.broadcasted_iota(jnp.int32, parent.shape, 0)
    rank = jnp.zeros_like(parent)
    for p in range(PROB - 1):
        sibling = (parent == parent[:, p : p + 1]) & (problem_ids > p)
        rank = rank + jnp.where(sibling, 1, 0)
    rank_v[...] = rank
    places = lax.broadcasted_iota(jnp.int32, (beams, LANES), 1)
    to_send = jnp.zeros((beams, LANES), jnp.int32)
    to_serve = jnp.zeros((beams, LANES), jnp.int32)
    live = jnp.zeros((beams, LANES), jnp.int32)
    for beam in range(resident):
        own = pl.ds(me * resident + beam, 1)
        own_parent, own_rank, own_length = parent_v[own, :], rank_v[own, :], length_v[own, :]
        for k in range(CAP):
            here = places == beam * CAP + k
            match = (own_parent == beam_ids) & (own_rank == k)
            found = jnp.sum(jnp.where(match, problem_ids, 0), axis=1, keepdims=True)
            to_send = jnp.where(here, found, to_send)
            match = (parent == me * resident + beam) & (rank == k)
            found = jnp.sum(jnp.where(match, problem_ids, 0), axis=1, keepdims=True)
            to_serve = jnp.where(here, found, to_serve)
            found = jnp.sum(jnp.where(match, own_length, 0), axis=1, keepdims=True)
            live = jnp.where(here, found, live)
    table_v[0:beams, :] = to_send
    table_v[beams : 2 * beams, :] = to_serve
    table_v[2 * beams : 3 * beams, :] = live
    table_v[3 * beams : 4 * beams, 0:PROB] = rank
    table_v[4 * beams : 5 * beams, 0:PROB] = parent
    to_scalar = pltpu.make_async_copy(table_v, table, small_sem.at[4])
    to_scalar.start()
    to_scalar.wait()

    pl.semaphore_wait(barrier, n)

    @pl.loop(1, n)
    def _(step):
        peer = lax.rem(me + step, n)
        pack(peer, sent_q)
        query_copy(peer, me).start()

    pack(me, got_q)

    spread_row = lax.broadcasted_iota(jnp.int32, (heads, width), 0)
    spread_col = lax.broadcasted_iota(jnp.int32, (heads, width), 1)
    block_mask = jnp.zeros((heads, width), jnp.float32)
    for k in range(kv_heads):
        inside = (
            (spread_row >= k * group)
            & (spread_row < (k + 1) * group)
            & (spread_col >= k * HEAD)
            & (spread_col < (k + 1) * HEAD)
        )
        block_mask = jnp.where(inside, 1.0, block_mask)
    block_mask = block_mask.astype(jnp.bfloat16)
    stat_row = lax.broadcasted_iota(jnp.int32, (heads, LANES), 0)
    stat_col = lax.broadcasted_iota(jnp.int32, (heads, LANES), 1)

    for chunk in range(chunks):
        load(0, chunk).wait()
    own_batch = 8

    @pl.loop(0, rows // own_batch)
    def _(batch):
        places = [batch * own_batch + i for i in range(own_batch)]
        results = attend_group(
            [queries[j] for j in places],
            [step_v[j, :STEP, :] for j in places],
            [step_v[j, STEP:, :] for j in places],
            [bounds_smem[lax.div(j, PROB), lax.rem(j, PROB)] + 1 for j in places],
            block_mask,
        )
        for j, (numerator, maxima, totals) in zip(places, results):
            own_num[j] = numerator
            own_max[j] = jnp.broadcast_to(maxima, (heads, LANES))
            own_tot[j] = jnp.broadcast_to(totals, (heads, LANES))

    for chunk in range(chunks):
        load(1, chunk).wait()

    def serve(peer, reply, stats):
        batch = 6 if slots % 6 == 0 else slots
        for first in range(0, slots, batch):
            numbers = range(first, first + batch)
            cells = [
                (
                    peer * resident + slot // (resident * CAP),
                    slot // CAP % resident * CAP + slot % CAP,
                )
                for slot in numbers
            ]
            places = [
                slot // CAP % resident * PROB + table[beams + row, cell]
                for slot, (row, cell) in zip(numbers, cells)
            ]
            results = attend_group(
                [got_q[peer, slot] for slot in numbers],
                [cache_v[j, :CTX, :] for j in places],
                [cache_v[j, CTX:, :] for j in places],
                [table[2 * beams + row, cell] for row, cell in cells],
                block_mask,
            )
            for slot, (numerator, maxima, totals) in zip(numbers, results):
                largest = jnp.max(jnp.abs(numerator), axis=-1, keepdims=True)
                largest = jnp.maximum(largest, 1e-20)
                coded = jnp.round(numerator * (CODES / largest))
                reply[peer, slot] = coded.astype(jnp.int32).astype(jnp.int16)
                packed = jnp.where(stat_col == stat_row, maxima, 0.0)
                packed = jnp.where(stat_col == stat_row + heads, totals, packed)
                packed = jnp.where(stat_col == stat_row + 2 * heads, largest, packed)
                stats[peer, slot : slot + 1, :] = jnp.sum(packed, axis=0, keepdims=True)

    serve(me, got_r, got_s)

    @pl.loop(1, n)
    def _(step):
        peer = lax.rem(me + n - step, n)
        query_copy(peer, peer).wait_recv()
        serve(peer, sent_r, sent_s)
        reply_copy(peer, me).start()
        stat_copy(peer, me).start()

    for chunk in range(chunks):
        load(2, chunk).wait()
    small[2].wait()
    small[3].wait()
    scaled = gain_v[...] * weight_v[...]
    lane = lax.broadcasted_iota(jnp.int32, (1, LANES), 1)
    last_row = jnp.zeros((1, LANES), jnp.int32)
    for j in range(rows):
        last_row = jnp.where(lane == j, bounds_smem[j // PROB, j % PROB], last_row)
    column = lax.broadcasted_iota(jnp.int32, (STEP, LANES), 1)

    def reward(j, carry):
        squares_all, products_all = carry
        wide = hidden_v[j].astype(jnp.float32)
        squares = jnp.sum(wide * wide, axis=-1, keepdims=True)
        products = jnp.sum(wide * scaled, axis=-1, keepdims=True)
        return (
            jnp.where(column == j, squares, squares_all),
            jnp.where(column == j, products, products_all),
        )

    zeros = jnp.zeros((STEP, LANES), jnp.float32)
    squares, products = lax.fori_loop(0, rows, reward, (zeros, zeros))
    part[0] = squares
    part[1] = products
    pair = pltpu.make_async_remote_copy(
        src_ref=part,
        dst_ref=other,
        send_sem=pair_sem.at[0],
        recv_sem=pair_sem.at[1],
        device_id={"tensor": 1 - core},
        device_id_type=MESH,
    )
    pair.start()
    pair.wait()
    squares = part[0] + other[0]
    products = part[1] + other[1]
    token_score = products / jnp.sqrt(squares / D_PRM + 1e-05)
    step_rows = lax.broadcasted_iota(jnp.int32, (STEP, LANES), 0)
    token_score = jnp.where(step_rows <= last_row, token_score, -1e30)
    best = jnp.max(token_score, axis=0, keepdims=True)
    for beam in range(resident):
        prm[beam : beam + 1, :] = best[:, beam * PROB : (beam + 1) * PROB]

    @pl.loop(1, n)
    def _(step):
        peer = lax.rem(me + n - step, n)
        reply_copy(peer, peer).wait_recv()
        stat_copy(peer, peer).wait_recv()

    merge_batch = 4

    @pl.loop(0, rows // merge_batch)
    def _(batch):
        for i in range(merge_batch):
            j = batch * merge_batch + i
            beam, problem = lax.div(j, PROB), lax.rem(j, PROB)
            ancestor = table[4 * beams + me * resident + beam, problem]
            place = jnp.minimum(table[3 * beams + me * resident + beam, problem], CAP - 1)
            source = lax.div(ancestor, resident)
            slot = (beam * resident + lax.rem(ancestor, resident)) * CAP + place
            stats = got_s[source, pl.ds(slot, 1), :]
            cache_max = jnp.sum(
                jnp.where(stat_col == stat_row, stats, 0.0), axis=-1, keepdims=True
            )
            cache_tot = jnp.sum(
                jnp.where(stat_col == stat_row + heads, stats, 0.0), axis=-1, keepdims=True
            )
            cache_step = jnp.sum(
                jnp.where(stat_col == stat_row + 2 * heads, stats, 0.0), axis=-1, keepdims=True
            ) * (1.0 / CODES)
            highest = jnp.maximum(cache_max, own_max[j])
            scale_cache = jnp.exp(cache_max - highest)
            scale_own = jnp.exp(own_max[j] - highest)
            totals = cache_tot * scale_cache + own_tot[j] * scale_own
            coded = got_r[source, slot].astype(jnp.int32).astype(jnp.float32)
            cache_num = coded * (cache_step * scale_cache)
            merged = (cache_num + own_num[j] * scale_own) / totals
            out[j] = merged.astype(jnp.bfloat16)

    @pl.loop(1, n)
    def _(step):
        peer = lax.rem(me + step, n)
        query_copy(peer, me).wait_send()
        reply_copy(peer, me).wait_send()
        stat_copy(peer, me).wait_send()


def body(
    n,
    step_hidden,
    prm_gain,
    score_weight,
    step_bounds,
    queries,
    step_kv,
    caches,
    parents,
    lengths,
):
    resident = step_hidden.shape[0]
    rows = resident * PROB
    slots = resident * resident * CAP
    heads = queries.shape[-1] // HEAD
    width = caches.shape[-1]
    beams = parents.shape[0]
    smem = pl.BlockSpec(memory_space=pltpu.SMEM)
    vmem = pl.BlockSpec(memory_space=pltpu.VMEM)
    hbm = pl.BlockSpec(memory_space=pl.ANY)
    chunks = 4
    dma = pltpu.SemaphoreType.DMA
    attended, prm = pl.pallas_call(
        functools.partial(kernel, n, resident),
        out_shape=(
            jax.ShapeDtypeStruct((rows, heads, HEAD), jnp.bfloat16),
            jax.ShapeDtypeStruct((resident, PROB), jnp.float32),
        ),
        in_specs=[smem, vmem] + [hbm] * 7,
        out_specs=(vmem, vmem),
        scratch_shapes=[
            pltpu.VMEM((1, prm_gain.shape[0]), jnp.float32),
            pltpu.VMEM((1, prm_gain.shape[0]), jnp.float32),
            pltpu.VMEM((beams, PROB), jnp.int32),
            pltpu.VMEM((beams, PROB), jnp.int32),
            pltpu.VMEM((beams, PROB), jnp.int32),
            pltpu.VMEM((5 * beams, LANES), jnp.int32),
            pltpu.SMEM((5 * beams, LANES), jnp.int32),
            pltpu.VMEM((rows, STEP, step_hidden.shape[-1]), jnp.bfloat16),
            pltpu.VMEM((rows, 2 * STEP, width), jnp.bfloat16),
            pltpu.VMEM((rows, 2 * CTX, width), jnp.bfloat16),
            pltpu.VMEM((n, slots, heads, HEAD), jnp.bfloat16),
            pltpu.VMEM((n, slots, heads, HEAD), jnp.bfloat16),
            pltpu.VMEM((n, slots, heads, HEAD), jnp.int16),
            pltpu.VMEM((n, slots, heads, HEAD), jnp.int16),
            pltpu.VMEM((n, -(-slots // 8) * 8, LANES), jnp.float32),
            pltpu.VMEM((n, -(-slots // 8) * 8, LANES), jnp.float32),
            pltpu.VMEM((rows, heads, HEAD), jnp.float32),
            pltpu.VMEM((rows, heads, LANES), jnp.float32),
            pltpu.VMEM((rows, heads, LANES), jnp.float32),
            pltpu.VMEM((2, STEP, LANES), jnp.float32),
            pltpu.VMEM((2, STEP, LANES), jnp.float32),
            dma((5,)),
            dma((3, chunks)),
            dma((n,)),
            dma((n,)),
            dma((n,)),
            dma((n,)),
            dma((n,)),
            dma((n,)),
            dma((2,)),
        ],
        compiler_params=pltpu.CompilerParams(
            collective_id=0, has_side_effects=True, vmem_limit_bytes=60 * 1024 * 1024
        ),
    )(
        step_bounds,
        queries.reshape(rows, heads, HEAD),
        prm_gain.reshape(1, -1),
        score_weight.reshape(1, -1),
        parents[:, :, 0],
        lengths,
        step_hidden.reshape(rows, STEP, step_hidden.shape[-1]),
        step_kv.reshape(rows, 2 * STEP, width),
        caches.reshape(rows, 2 * CTX, width),
    )
    attended = attended.reshape(resident, PROB, heads * HEAD)
    return attended, prm


def solution(mesh):
    in_specs = (
        P("dp", "groups", None, "tensor"),
        P("tensor"),
        P("tensor"),
        P("dp", "groups"),
        P("dp", "groups", "tensor"),
        P("dp", "groups", None, None, "tensor"),
        P("dp", "groups", None, None, "tensor"),
        P(None, "groups", None),
        P(None, "groups"),
    )
    out_specs = (P("dp", "groups", "tensor"), P("dp", "groups"))
    return jax.shard_map(
        functools.partial(body, mesh.shape["dp"]),
        mesh=mesh,
        in_specs=in_specs,
        out_specs=out_specs,
        check_vma=False,
    )
```

```python
import functools
import math

import jax
import jax.numpy as jnp
from jax import lax
from jax.experimental import pallas as pl
from jax.experimental.pallas import tpu as pltpu
from jax.sharding import PartitionSpec as P

HEAD = 128
D_PRM = 4096
PROB = 16
CTX = 128
STEP = 64
CAP = 3
LANES = 128
CODES = 32767.0
MESH = pl.DeviceIdType.MESH


def attend_group(queries, keys, values, limits, block_mask):
    heads = queries[0].shape[0]
    kv_heads = keys[0].shape[1] // HEAD
    group = heads // kv_heads
    count = len(queries)
    scores = []
    for query, key, limit in zip(queries, keys, limits):
        spread = jnp.concatenate([query] * kv_heads, axis=1) * block_mask
        score = lax.dot_general(
            spread, key, (((1,), (1,)), ((), ())), preferred_element_type=jnp.float32
        ) * (1.0 / math.sqrt(HEAD))
        column = lax.broadcasted_iota(jnp.int32, score.shape, 1)
        scores.append(jnp.where(column < limit, score, -1e30))
    scores = jnp.concatenate(scores, axis=0)
    maxima = jnp.max(scores, axis=-1, keepdims=True)
    weights = jnp.exp(scores - maxima)
    totals = jnp.sum(weights, axis=-1, keepdims=True)
    high = weights.astype(jnp.bfloat16)
    low = (weights - high.astype(jnp.float32)).astype(jnp.bfloat16)
    results = []
    for i in range(count):
        rows = slice(i * heads, (i + 1) * heads)
        both = jnp.concatenate([high[rows], low[rows]], axis=0)
        product = lax.dot_general(
            both, values[i], (((1,), (0,)), ((), ())), preferred_element_type=jnp.float32
        )
        product = product[:heads] + product[heads:]
        numerator = jnp.concatenate(
            [
                product[k * group : (k + 1) * group, k * HEAD : (k + 1) * HEAD]
                for k in range(kv_heads)
            ],
            axis=0,
        )
        results.append((numerator, maxima[rows], totals[rows]))
    return results


def kernel(
    n,
    resident,
    bounds_smem,
    queries,
    gain,
    weight,
    parents,
    lengths,
    hidden,
    step_kv,
    caches,
    out,
    prm,
    gain_v,
    weight_v,
    parent_v,
    length_v,
    rank_v,
    table_v,
    table,
    hidden_v,
    step_v,
    cache_v,
    sent_q,
    got_q,
    sent_r,
    got_r,
    sent_s,
    got_s,
    own_num,
    own_max,
    own_tot,
    part,
    other,
    small_sem,
    load_sem,
    qs_sem,
    qr_sem,
    rs_sem,
    rr_sem,
    ss_sem,
    sr_sem,
    pair_sem,
):
    me = lax.axis_index("dp")
    core = lax.axis_index("tensor")
    rows = resident * PROB
    slots = resident * resident * CAP
    heads = queries.shape[1]
    width = step_v.shape[2]
    kv_heads = width // HEAD
    group = heads // kv_heads
    beams = n * resident

    chunks = load_sem.shape[1]
    span = rows // chunks

    def load(which, chunk):
        source, target = ((step_kv, step_v), (caches, cache_v), (hidden, hidden_v))[which]
        piece = pl.ds(chunk * span, span)
        return pltpu.make_async_copy(
            source.at[piece], target.at[piece], load_sem.at[which, chunk]
        )

    small = [
        pltpu.make_async_copy(source, target, small_sem.at[i])
        for i, (source, target) in enumerate(
            ((parents, parent_v), (lengths, length_v), (gain, gain_v), (weight, weight_v))
        )
    ]
    for copy in small:
        copy.start()
    for which in range(3):
        for chunk in range(chunks):
            load(which, chunk).start()

    barrier = pltpu.get_barrier_semaphore()
    for step in range(1, n):
        pl.semaphore_signal(
            barrier, inc=1, device_id={"dp": lax.rem(me + step, n)}, device_id_type=MESH
        )
    pl.semaphore_signal(barrier, inc=1, device_id={"tensor": 1 - core}, device_id_type=MESH)

    def offset(step):
        return n // 2 + lax.div(step, 2) * (2 * lax.rem(step, 2) - 1)

    def query_copy(peer, source):
        return pltpu.make_async_remote_copy(
            src_ref=sent_q.at[peer],
            dst_ref=got_q.at[source],
            send_sem=qs_sem.at[peer],
            recv_sem=qr_sem.at[source],
            device_id={"dp": peer},
            device_id_type=MESH,
        )

    def reply_copy(peer, source):
        return pltpu.make_async_remote_copy(
            src_ref=sent_r.at[peer],
            dst_ref=got_r.at[source],
            send_sem=rs_sem.at[peer],
            recv_sem=rr_sem.at[source],
            device_id={"dp": peer},
            device_id_type=MESH,
        )

    def stat_copy(peer, source):
        return pltpu.make_async_remote_copy(
            src_ref=sent_s.at[peer],
            dst_ref=got_s.at[source],
            send_sem=ss_sem.at[peer],
            recv_sem=sr_sem.at[source],
            device_id={"dp": peer},
            device_id_type=MESH,
        )

    def pack(peer, target):
        for slot in range(slots):
            beam = slot // (resident * CAP)
            near = slot // CAP % resident
            problem = table[peer * resident + near, beam * CAP + slot % CAP]
            target[peer, slot] = queries[beam * PROB + problem]

    small[0].wait()
    small[1].wait()
    table_v[...] = jnp.zeros_like(table_v)
    parent = parent_v[...]
    problem_ids = lax.broadcasted_iota(jnp.int32, parent.shape, 1)
    beam_ids = lax.broadcasted_iota(jnp.int32, parent.shape, 0)
    rank = jnp.zeros_like(parent)
    for p in range(PROB - 1):
        sibling = (parent == parent[:, p : p + 1]) & (problem_ids > p)
        rank = rank + jnp.where(sibling, 1, 0)
    rank_v[...] = rank
    places = lax.broadcasted_iota(jnp.int32, (beams, LANES), 1)
    to_send = jnp.zeros((beams, LANES), jnp.int32)
    to_serve = jnp.zeros((beams, LANES), jnp.int32)
    live = jnp.zeros((beams, LANES), jnp.int32)
    for beam in range(resident):
        own = pl.ds(me * resident + beam, 1)
        own_parent, own_rank, own_length = parent_v[own, :], rank_v[own, :], length_v[own, :]
        for k in range(CAP):
            here = places == beam * CAP + k
            match = (own_parent == beam_ids) & (own_rank == k)
            found = jnp.sum(jnp.where(match, problem_ids, 0), axis=1, keepdims=True)
            to_send = jnp.where(here, found, to_send)
            match = (parent == me * resident + beam) & (rank == k)
            found = jnp.sum(jnp.where(match, problem_ids, 0), axis=1, keepdims=True)
            to_serve = jnp.where(here, found, to_serve)
            found = jnp.sum(jnp.where(match, own_length, 0), axis=1, keepdims=True)
            live = jnp.where(here, found, live)
    table_v[0:beams, :] = to_send
    table_v[beams : 2 * beams, :] = to_serve
    table_v[2 * beams : 3 * beams, :] = live
    table_v[3 * beams : 4 * beams, 0:PROB] = rank
    table_v[4 * beams : 5 * beams, 0:PROB] = parent
    to_scalar = pltpu.make_async_copy(table_v, table, small_sem.at[4])
    to_scalar.start()
    to_scalar.wait()

    pl.semaphore_wait(barrier, n)

    @pl.loop(1, n)
    def _(step):
        peer = lax.rem(me + offset(step), n)
        pack(peer, sent_q)
        query_copy(peer, me).start()

    pack(me, got_q)

    spread_row = lax.broadcasted_iota(jnp.int32, (heads, width), 0)
    spread_col = lax.broadcasted_iota(jnp.int32, (heads, width), 1)
    block_mask = jnp.zeros((heads, width), jnp.float32)
    for k in range(kv_heads):
        inside = (
            (spread_row >= k * group)
            & (spread_row < (k + 1) * group)
            & (spread_col >= k * HEAD)
            & (spread_col < (k + 1) * HEAD)
        )
        block_mask = jnp.where(inside, 1.0, block_mask)
    block_mask = block_mask.astype(jnp.bfloat16)
    stat_row = lax.broadcasted_iota(jnp.int32, (heads, LANES), 0)
    stat_col = lax.broadcasted_iota(jnp.int32, (heads, LANES), 1)

    for chunk in range(chunks):
        load(0, chunk).wait()
    own_batch = 8

    @pl.loop(0, rows // own_batch)
    def _(batch):
        places = [batch * own_batch + i for i in range(own_batch)]
        results = attend_group(
            [queries[j] for j in places],
            [step_v[j, :STEP, :] for j in places],
            [step_v[j, STEP:, :] for j in places],
            [bounds_smem[lax.div(j, PROB), lax.rem(j, PROB)] + 1 for j in places],
            block_mask,
        )
        for j, (numerator, maxima, totals) in zip(places, results):
            own_num[j] = numerator
            own_max[j] = jnp.broadcast_to(maxima, (heads, LANES))
            own_tot[j] = jnp.broadcast_to(totals, (heads, LANES))

    for chunk in range(chunks):
        load(1, chunk).wait()

    def serve(peer, reply, stats):
        batch = 6 if slots % 6 == 0 else slots
        for first in range(0, slots, batch):
            numbers = range(first, first + batch)
            cells = [
                (
                    peer * resident + slot // (resident * CAP),
                    slot // CAP % resident * CAP + slot % CAP,
                )
                for slot in numbers
            ]
            places = [
                slot // CAP % resident * PROB + table[beams + row, cell]
                for slot, (row, cell) in zip(numbers, cells)
            ]
            results = attend_group(
                [got_q[peer, slot] for slot in numbers],
                [cache_v[j, :CTX, :] for j in places],
                [cache_v[j, CTX:, :] for j in places],
                [table[2 * beams + row, cell] for row, cell in cells],
                block_mask,
            )
            for slot, (numerator, maxima, totals) in zip(numbers, results):
                largest = jnp.max(jnp.abs(numerator), axis=-1, keepdims=True)
                largest = jnp.maximum(largest, 1e-20)
                coded = jnp.round(numerator * (CODES / largest))
                reply[peer, slot] = coded.astype(jnp.int32).astype(jnp.int16)
                packed = jnp.where(stat_col == stat_row, maxima, 0.0)
                packed = jnp.where(stat_col == stat_row + heads, totals, packed)
                packed = jnp.where(stat_col == stat_row + 2 * heads, largest, packed)
                stats[peer, slot : slot + 1, :] = jnp.sum(packed, axis=0, keepdims=True)

    serve(me, got_r, got_s)

    @pl.loop(1, n)
    def _(step):
        peer = lax.rem(me + n - offset(step), n)
        query_copy(peer, peer).wait_recv()
        serve(peer, sent_r, sent_s)
        reply_copy(peer, me).start()
        stat_copy(peer, me).start()

    for chunk in range(chunks):
        load(2, chunk).wait()
    small[2].wait()
    small[3].wait()
    scaled = gain_v[...] * weight_v[...]
    lane = lax.broadcasted_iota(jnp.int32, (1, LANES), 1)
    last_row = jnp.zeros((1, LANES), jnp.int32)
    for j in range(rows):
        last_row = jnp.where(lane == j, bounds_smem[j // PROB, j % PROB], last_row)
    column = lax.broadcasted_iota(jnp.int32, (STEP, LANES), 1)

    def reward(j, carry):
        squares_all, products_all = carry
        wide = hidden_v[j].astype(jnp.float32)
        squares = jnp.sum(wide * wide, axis=-1, keepdims=True)
        products = jnp.sum(wide * scaled, axis=-1, keepdims=True)
        return (
            jnp.where(column == j, squares, squares_all),
            jnp.where(column == j, products, products_all),
        )

    zeros = jnp.zeros((STEP, LANES), jnp.float32)
    squares, products = lax.fori_loop(0, rows, reward, (zeros, zeros))
    part[0] = squares
    part[1] = products
    pair = pltpu.make_async_remote_copy(
        src_ref=part,
        dst_ref=other,
        send_sem=pair_sem.at[0],
        recv_sem=pair_sem.at[1],
        device_id={"tensor": 1 - core},
        device_id_type=MESH,
    )
    pair.start()
    pair.wait()
    squares = part[0] + other[0]
    products = part[1] + other[1]
    token_score = products / jnp.sqrt(squares / D_PRM + 1e-05)
    step_rows = lax.broadcasted_iota(jnp.int32, (STEP, LANES), 0)
    token_score = jnp.where(step_rows <= last_row, token_score, -1e30)
    best = jnp.max(token_score, axis=0, keepdims=True)
    for beam in range(resident):
        prm[beam : beam + 1, :] = best[:, beam * PROB : (beam + 1) * PROB]

    @pl.loop(1, n)
    def _(step):
        peer = lax.rem(me + n - step, n)
        reply_copy(peer, peer).wait_recv()
        stat_copy(peer, peer).wait_recv()

    merge_batch = 4

    @pl.loop(0, rows // merge_batch)
    def _(batch):
        for i in range(merge_batch):
            j = batch * merge_batch + i
            beam, problem = lax.div(j, PROB), lax.rem(j, PROB)
            ancestor = table[4 * beams + me * resident + beam, problem]
            place = jnp.minimum(table[3 * beams + me * resident + beam, problem], CAP - 1)
            source = lax.div(ancestor, resident)
            slot = (beam * resident + lax.rem(ancestor, resident)) * CAP + place
            stats = got_s[source, pl.ds(slot, 1), :]
            cache_max = jnp.sum(
                jnp.where(stat_col == stat_row, stats, 0.0), axis=-1, keepdims=True
            )
            cache_tot = jnp.sum(
                jnp.where(stat_col == stat_row + heads, stats, 0.0), axis=-1, keepdims=True
            )
            cache_step = jnp.sum(
                jnp.where(stat_col == stat_row + 2 * heads, stats, 0.0), axis=-1, keepdims=True
            ) * (1.0 / CODES)
            highest = jnp.maximum(cache_max, own_max[j])
            scale_cache = jnp.exp(cache_max - highest)
            scale_own = jnp.exp(own_max[j] - highest)
            totals = cache_tot * scale_cache + own_tot[j] * scale_own
            coded = got_r[source, slot].astype(jnp.int32).astype(jnp.float32)
            cache_num = coded * (cache_step * scale_cache)
            merged = (cache_num + own_num[j] * scale_own) / totals
            out[j] = merged.astype(jnp.bfloat16)

    @pl.loop(1, n)
    def _(step):
        peer = lax.rem(me + step, n)
        query_copy(peer, me).wait_send()
        reply_copy(peer, me).wait_send()
        stat_copy(peer, me).wait_send()


def body(
    n,
    step_hidden,
    prm_gain,
    score_weight,
    step_bounds,
    queries,
    step_kv,
    caches,
    parents,
    lengths,
):
    resident = step_hidden.shape[0]
    rows = resident * PROB
    slots = resident * resident * CAP
    heads = queries.shape[-1] // HEAD
    width = caches.shape[-1]
    beams = parents.shape[0]
    smem = pl.BlockSpec(memory_space=pltpu.SMEM)
    vmem = pl.BlockSpec(memory_space=pltpu.VMEM)
    hbm = pl.BlockSpec(memory_space=pl.ANY)
    chunks = 4
    dma = pltpu.SemaphoreType.DMA
    attended, prm = pl.pallas_call(
        functools.partial(kernel, n, resident),
        out_shape=(
            jax.ShapeDtypeStruct((rows, heads, HEAD), jnp.bfloat16),
            jax.ShapeDtypeStruct((resident, PROB), jnp.float32),
        ),
        in_specs=[smem, vmem] + [hbm] * 7,
        out_specs=(vmem, vmem),
        scratch_shapes=[
            pltpu.VMEM((1, prm_gain.shape[0]), jnp.float32),
            pltpu.VMEM((1, prm_gain.shape[0]), jnp.float32),
            pltpu.VMEM((beams, PROB), jnp.int32),
            pltpu.VMEM((beams, PROB), jnp.int32),
            pltpu.VMEM((beams, PROB), jnp.int32),
            pltpu.VMEM((5 * beams, LANES), jnp.int32),
            pltpu.SMEM((5 * beams, LANES), jnp.int32),
            pltpu.VMEM((rows, STEP, step_hidden.shape[-1]), jnp.bfloat16),
            pltpu.VMEM((rows, 2 * STEP, width), jnp.bfloat16),
            pltpu.VMEM((rows, 2 * CTX, width), jnp.bfloat16),
            pltpu.VMEM((n, slots, heads, HEAD), jnp.bfloat16),
            pltpu.VMEM((n, slots, heads, HEAD), jnp.bfloat16),
            pltpu.VMEM((n, slots, heads, HEAD), jnp.int16),
            pltpu.VMEM((n, slots, heads, HEAD), jnp.int16),
            pltpu.VMEM((n, -(-slots // 8) * 8, LANES), jnp.float32),
            pltpu.VMEM((n, -(-slots // 8) * 8, LANES), jnp.float32),
            pltpu.VMEM((rows, heads, HEAD), jnp.float32),
            pltpu.VMEM((rows, heads, LANES), jnp.float32),
            pltpu.VMEM((rows, heads, LANES), jnp.float32),
            pltpu.VMEM((2, STEP, LANES), jnp.float32),
            pltpu.VMEM((2, STEP, LANES), jnp.float32),
            dma((5,)),
            dma((3, chunks)),
            dma((n,)),
            dma((n,)),
            dma((n,)),
            dma((n,)),
            dma((n,)),
            dma((n,)),
            dma((2,)),
        ],
        compiler_params=pltpu.CompilerParams(
            collective_id=0, has_side_effects=True, vmem_limit_bytes=60 * 1024 * 1024
        ),
    )(
        step_bounds,
        queries.reshape(rows, heads, HEAD),
        prm_gain.reshape(1, -1),
        score_weight.reshape(1, -1),
        parents[:, :, 0],
        lengths,
        step_hidden.reshape(rows, STEP, step_hidden.shape[-1]),
        step_kv.reshape(rows, 2 * STEP, width),
        caches.reshape(rows, 2 * CTX, width),
    )
    attended = attended.reshape(resident, PROB, heads * HEAD)
    return attended, prm


def solution(mesh):
    in_specs = (
        P("dp", "groups", None, "tensor"),
        P("tensor"),
        P("tensor"),
        P("dp", "groups"),
        P("dp", "groups", "tensor"),
        P("dp", "groups", None, None, "tensor"),
        P("dp", "groups", None, None, "tensor"),
        P(None, "groups", None),
        P(None, "groups"),
    )
    out_specs = (P("dp", "groups", "tensor"), P("dp", "groups"))
    return jax.shard_map(
        functools.partial(body, mesh.shape["dp"]),
        mesh=mesh,
        in_specs=in_specs,
        out_specs=out_specs,
        check_vma=False,
    )
```

```python
import functools
import math

import jax
import jax.numpy as jnp
from jax import lax
from jax.experimental import pallas as pl
from jax.experimental.pallas import tpu as pltpu
from jax.sharding import PartitionSpec as P

HEAD = 128
D_PRM = 4096
PROB = 16
CTX = 128
STEP = 64
CAP = 3
LANES = 128
CODES = 32767.0
MESH = pl.DeviceIdType.MESH


def attend_group(queries, keys, values, limits, block_mask):
    heads = queries[0].shape[0]
    kv_heads = keys[0].shape[1] // HEAD
    group = heads // kv_heads
    count = len(queries)
    scores = []
    for query, key, limit in zip(queries, keys, limits):
        spread = jnp.concatenate([query] * kv_heads, axis=1) * block_mask
        score = lax.dot_general(
            spread, key, (((1,), (1,)), ((), ())), preferred_element_type=jnp.float32
        ) * (1.0 / math.sqrt(HEAD))
        column = lax.broadcasted_iota(jnp.int32, score.shape, 1)
        scores.append(jnp.where(column < limit, score, -1e30))
    scores = jnp.concatenate(scores, axis=0)
    maxima = jnp.max(scores, axis=-1, keepdims=True)
    weights = jnp.exp(scores - maxima)
    totals = jnp.sum(weights, axis=-1, keepdims=True)
    high = weights.astype(jnp.bfloat16)
    low = (weights - high.astype(jnp.float32)).astype(jnp.bfloat16)
    results = []
    for i in range(count):
        rows = slice(i * heads, (i + 1) * heads)
        both = jnp.concatenate([high[rows], low[rows]], axis=0)
        product = lax.dot_general(
            both, values[i], (((1,), (0,)), ((), ())), preferred_element_type=jnp.float32
        )
        product = product[:heads] + product[heads:]
        numerator = jnp.concatenate(
            [
                product[k * group : (k + 1) * group, k * HEAD : (k + 1) * HEAD]
                for k in range(kv_heads)
            ],
            axis=0,
        )
        results.append((numerator, maxima[rows], totals[rows]))
    return results


def kernel(
    n,
    resident,
    bounds_smem,
    queries,
    gain,
    weight,
    parents,
    lengths,
    hidden,
    step_kv,
    caches,
    out,
    prm,
    gain_v,
    weight_v,
    parent_v,
    length_v,
    rank_v,
    table_v,
    table,
    hidden_v,
    step_v,
    cache_v,
    sent_q,
    got_q,
    sent_r,
    got_r,
    sent_s,
    got_s,
    own_num,
    own_max,
    own_tot,
    part,
    other,
    small_sem,
    load_sem,
    qs_sem,
    qr_sem,
    rs_sem,
    rr_sem,
    ss_sem,
    sr_sem,
    pair_sem,
):
    me = lax.axis_index("dp")
    core = lax.axis_index("tensor")
    rows = resident * PROB
    slots = resident * resident * CAP
    heads = queries.shape[1]
    width = step_v.shape[2]
    kv_heads = width // HEAD
    group = heads // kv_heads
    beams = n * resident

    chunks = load_sem.shape[1]
    span = rows // chunks

    def load(which, chunk):
        source, target = ((step_kv, step_v), (caches, cache_v), (hidden, hidden_v))[which]
        piece = pl.ds(chunk * span, span)
        return pltpu.make_async_copy(
            source.at[piece], target.at[piece], load_sem.at[which, chunk]
        )

    small = [
        pltpu.make_async_copy(source, target, small_sem.at[i])
        for i, (source, target) in enumerate(
            ((parents, parent_v), (lengths, length_v), (gain, gain_v), (weight, weight_v))
        )
    ]
    for copy in small:
        copy.start()
    for which in range(3):
        for chunk in range(chunks):
            load(which, chunk).start()

    barrier = pltpu.get_barrier_semaphore()
    for step in range(1, n):
        pl.semaphore_signal(
            barrier, inc=1, device_id={"dp": lax.rem(me + step, n)}, device_id_type=MESH
        )
    pl.semaphore_signal(barrier, inc=1, device_id={"tensor": 1 - core}, device_id_type=MESH)

    def offset(step):
        return n // 2 + lax.div(step, 2) * (2 * lax.rem(step, 2) - 1)

    def query_copy(peer, source):
        return pltpu.make_async_remote_copy(
            src_ref=sent_q.at[peer],
            dst_ref=got_q.at[source],
            send_sem=qs_sem.at[peer],
            recv_sem=qr_sem.at[source],
            device_id={"dp": peer},
            device_id_type=MESH,
        )

    def reply_copy(peer, source):
        return pltpu.make_async_remote_copy(
            src_ref=sent_r.at[peer],
            dst_ref=got_r.at[source],
            send_sem=rs_sem.at[peer],
            recv_sem=rr_sem.at[source],
            device_id={"dp": peer},
            device_id_type=MESH,
        )

    def stat_copy(peer, source):
        return pltpu.make_async_remote_copy(
            src_ref=sent_s.at[peer],
            dst_ref=got_s.at[source],
            send_sem=ss_sem.at[peer],
            recv_sem=sr_sem.at[source],
            device_id={"dp": peer},
            device_id_type=MESH,
        )

    def pack(peer, target):
        for slot in range(slots):
            beam = slot // (resident * CAP)
            near = slot // CAP % resident
            problem = table[peer * resident + near, beam * CAP + slot % CAP]
            target[peer, slot] = queries[beam * PROB + problem]

    small[0].wait()
    small[1].wait()
    table_v[...] = jnp.zeros_like(table_v)
    parent = parent_v[...]
    problem_ids = lax.broadcasted_iota(jnp.int32, parent.shape, 1)
    beam_ids = lax.broadcasted_iota(jnp.int32, parent.shape, 0)
    rank = jnp.zeros_like(parent)
    for p in range(PROB - 1):
        sibling = (parent == parent[:, p : p + 1]) & (problem_ids > p)
        rank = rank + jnp.where(sibling, 1, 0)
    rank_v[...] = rank
    places = lax.broadcasted_iota(jnp.int32, (beams, LANES), 1)
    to_send = jnp.zeros((beams, LANES), jnp.int32)
    to_serve = jnp.zeros((beams, LANES), jnp.int32)
    live = jnp.zeros((beams, LANES), jnp.int32)
    for beam in range(resident):
        own = pl.ds(me * resident + beam, 1)
        own_parent, own_rank, own_length = parent_v[own, :], rank_v[own, :], length_v[own, :]
        for k in range(CAP):
            here = places == beam * CAP + k
            match = (own_parent == beam_ids) & (own_rank == k)
            found = jnp.sum(jnp.where(match, problem_ids, 0), axis=1, keepdims=True)
            to_send = jnp.where(here, found, to_send)
            match = (parent == me * resident + beam) & (rank == k)
            found = jnp.sum(jnp.where(match, problem_ids, 0), axis=1, keepdims=True)
            to_serve = jnp.where(here, found, to_serve)
            found = jnp.sum(jnp.where(match, own_length, 0), axis=1, keepdims=True)
            live = jnp.where(here, found, live)
    table_v[0:beams, :] = to_send
    table_v[beams : 2 * beams, :] = to_serve
    table_v[2 * beams : 3 * beams, :] = live
    table_v[3 * beams : 4 * beams, 0:PROB] = rank
    table_v[4 * beams : 5 * beams, 0:PROB] = parent
    to_scalar = pltpu.make_async_copy(table_v, table, small_sem.at[4])
    to_scalar.start()
    to_scalar.wait()

    pl.semaphore_wait(barrier, n)

    @pl.loop(1, n)
    def _(step):
        peer = lax.rem(me + offset(step), n)
        pack(peer, sent_q)
        query_copy(peer, me).start()

    pack(me, got_q)

    spread_row = lax.broadcasted_iota(jnp.int32, (heads, width), 0)
    spread_col = lax.broadcasted_iota(jnp.int32, (heads, width), 1)
    block_mask = jnp.zeros((heads, width), jnp.float32)
    for k in range(kv_heads):
        inside = (
            (spread_row >= k * group)
            & (spread_row < (k + 1) * group)
            & (spread_col >= k * HEAD)
            & (spread_col < (k + 1) * HEAD)
        )
        block_mask = jnp.where(inside, 1.0, block_mask)
    block_mask = block_mask.astype(jnp.bfloat16)
    stat_row = lax.broadcasted_iota(jnp.int32, (heads, LANES), 0)
    stat_col = lax.broadcasted_iota(jnp.int32, (heads, LANES), 1)

    for chunk in range(chunks):
        load(0, chunk).wait()
    own_batch = 8

    @pl.loop(0, rows // own_batch)
    def _(batch):
        places = [batch * own_batch + i for i in range(own_batch)]
        results = attend_group(
            [queries[j] for j in places],
            [step_v[j, :STEP, :] for j in places],
            [step_v[j, STEP:, :] for j in places],
            [bounds_smem[lax.div(j, PROB), lax.rem(j, PROB)] + 1 for j in places],
            block_mask,
        )
        for j, (numerator, maxima, totals) in zip(places, results):
            own_num[j] = numerator
            own_max[j] = jnp.broadcast_to(maxima, (heads, LANES))
            own_tot[j] = jnp.broadcast_to(totals, (heads, LANES))

    for chunk in range(chunks):
        load(1, chunk).wait()

    def serve(peer, reply, stats):
        batch = 6 if slots % 6 == 0 else slots
        for first in range(0, slots, batch):
            numbers = range(first, first + batch)
            cells = [
                (
                    peer * resident + slot // (resident * CAP),
                    slot // CAP % resident * CAP + slot % CAP,
                )
                for slot in numbers
            ]
            places = [
                slot // CAP % resident * PROB + table[beams + row, cell]
                for slot, (row, cell) in zip(numbers, cells)
            ]
            results = attend_group(
                [got_q[peer, slot] for slot in numbers],
                [cache_v[j, :CTX, :] for j in places],
                [cache_v[j, CTX:, :] for j in places],
                [table[2 * beams + row, cell] for row, cell in cells],
                block_mask,
            )
            for slot, (numerator, maxima, totals) in zip(numbers, results):
                largest = jnp.max(jnp.abs(numerator), axis=-1, keepdims=True)
                largest = jnp.maximum(largest, 1e-20)
                coded = jnp.round(numerator * (CODES / largest))
                reply[peer, slot] = coded.astype(jnp.int32).astype(jnp.int16)
                packed = jnp.where(stat_col == stat_row, maxima, 0.0)
                packed = jnp.where(stat_col == stat_row + heads, totals, packed)
                packed = jnp.where(stat_col == stat_row + 2 * heads, largest, packed)
                stats[peer, slot : slot + 1, :] = jnp.sum(packed, axis=0, keepdims=True)

    serve(me, got_r, got_s)

    @pl.loop(1, n)
    def _(step):
        peer = lax.rem(me + n - offset(step), n)
        query_copy(peer, peer).wait_recv()
        serve(peer, sent_r, sent_s)
        reply_copy(peer, me).start()
        stat_copy(peer, me).start()

    for chunk in range(chunks):
        load(2, chunk).wait()
    small[2].wait()
    small[3].wait()
    scaled = gain_v[...] * weight_v[...]
    lane = lax.broadcasted_iota(jnp.int32, (1, LANES), 1)
    last_row = jnp.zeros((1, LANES), jnp.int32)
    for j in range(rows):
        last_row = jnp.where(lane == j, bounds_smem[j // PROB, j % PROB], last_row)
    column = lax.broadcasted_iota(jnp.int32, (STEP, LANES), 1)

    def reward(j, carry):
        squares_all, products_all = carry
        wide = hidden_v[j].astype(jnp.float32)
        squares = jnp.sum(wide * wide, axis=-1, keepdims=True)
        products = jnp.sum(wide * scaled, axis=-1, keepdims=True)
        return (
            jnp.where(column == j, squares, squares_all),
            jnp.where(column == j, products, products_all),
        )

    zeros = jnp.zeros((STEP, LANES), jnp.float32)
    squares, products = lax.fori_loop(0, rows, reward, (zeros, zeros))
    part[0] = squares
    part[1] = products
    pair = pltpu.make_async_remote_copy(
        src_ref=part,
        dst_ref=other,
        send_sem=pair_sem.at[0],
        recv_sem=pair_sem.at[1],
        device_id={"tensor": 1 - core},
        device_id_type=MESH,
    )
    pair.start()
    pair.wait()
    squares = part[0] + other[0]
    products = part[1] + other[1]
    token_score = products / jnp.sqrt(squares / D_PRM + 1e-05)
    step_rows = lax.broadcasted_iota(jnp.int32, (STEP, LANES), 0)
    token_score = jnp.where(step_rows <= last_row, token_score, -1e30)
    prm[...] = jnp.max(token_score, axis=0, keepdims=True)

    @pl.loop(1, n)
    def _(step):
        peer = lax.rem(me + n - step, n)
        reply_copy(peer, peer).wait_recv()
        stat_copy(peer, peer).wait_recv()

    merge_batch = 4

    @pl.loop(0, rows // merge_batch)
    def _(batch):
        for i in range(merge_batch):
            j = batch * merge_batch + i
            beam, problem = lax.div(j, PROB), lax.rem(j, PROB)
            ancestor = table[4 * beams + me * resident + beam, problem]
            place = jnp.minimum(table[3 * beams + me * resident + beam, problem], CAP - 1)
            source = lax.div(ancestor, resident)
            slot = (beam * resident + lax.rem(ancestor, resident)) * CAP + place
            stats = got_s[source, pl.ds(slot, 1), :]
            cache_max = jnp.sum(
                jnp.where(stat_col == stat_row, stats, 0.0), axis=-1, keepdims=True
            )
            cache_tot = jnp.sum(
                jnp.where(stat_col == stat_row + heads, stats, 0.0), axis=-1, keepdims=True
            )
            cache_step = jnp.sum(
                jnp.where(stat_col == stat_row + 2 * heads, stats, 0.0), axis=-1, keepdims=True
            ) * (1.0 / CODES)
            highest = jnp.maximum(cache_max, own_max[j])
            scale_cache = jnp.exp(cache_max - highest)
            scale_own = jnp.exp(own_max[j] - highest)
            totals = cache_tot * scale_cache + own_tot[j] * scale_own
            coded = got_r[source, slot].astype(jnp.int32).astype(jnp.float32)
            cache_num = coded * (cache_step * scale_cache)
            merged = (cache_num + own_num[j] * scale_own) / totals
            out[j] = merged.astype(jnp.bfloat16)

    @pl.loop(1, n)
    def _(step):
        peer = lax.rem(me + step, n)
        query_copy(peer, me).wait_send()
        reply_copy(peer, me).wait_send()
        stat_copy(peer, me).wait_send()


def body(
    n,
    step_hidden,
    prm_gain,
    score_weight,
    step_bounds,
    queries,
    step_kv,
    caches,
    parents,
    lengths,
):
    resident = step_hidden.shape[0]
    rows = resident * PROB
    slots = resident * resident * CAP
    heads = queries.shape[-1] // HEAD
    width = caches.shape[-1]
    beams = parents.shape[0]
    smem = pl.BlockSpec(memory_space=pltpu.SMEM)
    vmem = pl.BlockSpec(memory_space=pltpu.VMEM)
    hbm = pl.BlockSpec(memory_space=pl.ANY)
    chunks = 4
    dma = pltpu.SemaphoreType.DMA
    attended, prm = pl.pallas_call(
        functools.partial(kernel, n, resident),
        out_shape=(
            jax.ShapeDtypeStruct((rows, heads, HEAD), jnp.bfloat16),
            jax.ShapeDtypeStruct((1, LANES), jnp.float32),
        ),
        in_specs=[smem, vmem] + [hbm] * 7,
        out_specs=(vmem, vmem),
        scratch_shapes=[
            pltpu.VMEM((1, prm_gain.shape[0]), jnp.float32),
            pltpu.VMEM((1, prm_gain.shape[0]), jnp.float32),
            pltpu.VMEM((beams, PROB), jnp.int32),
            pltpu.VMEM((beams, PROB), jnp.int32),
            pltpu.VMEM((beams, PROB), jnp.int32),
            pltpu.VMEM((5 * beams, LANES), jnp.int32),
            pltpu.SMEM((5 * beams, LANES), jnp.int32),
            pltpu.VMEM((rows, STEP, step_hidden.shape[-1]), jnp.bfloat16),
            pltpu.VMEM((rows, 2 * STEP, width), jnp.bfloat16),
            pltpu.VMEM((rows, 2 * CTX, width), jnp.bfloat16),
            pltpu.VMEM((n, slots, heads, HEAD), jnp.bfloat16),
            pltpu.VMEM((n, slots, heads, HEAD), jnp.bfloat16),
            pltpu.VMEM((n, slots, heads, HEAD), jnp.int16),
            pltpu.VMEM((n, slots, heads, HEAD), jnp.int16),
            pltpu.VMEM((n, -(-slots // 8) * 8, LANES), jnp.float32),
            pltpu.VMEM((n, -(-slots // 8) * 8, LANES), jnp.float32),
            pltpu.VMEM((rows, heads, HEAD), jnp.float32),
            pltpu.VMEM((rows, heads, LANES), jnp.float32),
            pltpu.VMEM((rows, heads, LANES), jnp.float32),
            pltpu.VMEM((2, STEP, LANES), jnp.float32),
            pltpu.VMEM((2, STEP, LANES), jnp.float32),
            dma((5,)),
            dma((3, chunks)),
            dma((n,)),
            dma((n,)),
            dma((n,)),
            dma((n,)),
            dma((n,)),
            dma((n,)),
            dma((2,)),
        ],
        compiler_params=pltpu.CompilerParams(
            collective_id=0, has_side_effects=True, vmem_limit_bytes=54400 * 1024
        ),
    )(
        step_bounds,
        queries.reshape(rows, heads, HEAD),
        prm_gain.reshape(1, -1),
        score_weight.reshape(1, -1),
        parents[:, :, 0],
        lengths,
        step_hidden.reshape(rows, STEP, step_hidden.shape[-1]),
        step_kv.reshape(rows, 2 * STEP, width),
        caches.reshape(rows, 2 * CTX, width),
    )
    attended = attended.reshape(resident, PROB, heads * HEAD)
    return attended, prm[0, :rows].reshape(resident, PROB)


def solution(mesh):
    in_specs = (
        P("dp", "groups", None, "tensor"),
        P("tensor"),
        P("tensor"),
        P("dp", "groups"),
        P("dp", "groups", "tensor"),
        P("dp", "groups", None, None, "tensor"),
        P("dp", "groups", None, None, "tensor"),
        P(None, "groups", None),
        P(None, "groups"),
    )
    out_specs = (P("dp", "groups", "tensor"), P("dp", "groups"))
    return jax.shard_map(
        functools.partial(body, mesh.shape["dp"]),
        mesh=mesh,
        in_specs=in_specs,
        out_specs=out_specs,
        check_vma=False,
    )
```

```python
import functools
import math

import jax
import jax.numpy as jnp
from jax import lax
from jax.experimental import pallas as pl
from jax.experimental.pallas import tpu as pltpu
from jax.sharding import PartitionSpec as P

HEAD = 128
D_PRM = 4096
PROB = 16
CTX = 128
STEP = 64
CAP = 3
LANES = 128
CODES = 32767.0
MESH = pl.DeviceIdType.MESH


def attend_group(queries, keys, values, limits, block_mask):
    heads = queries[0].shape[0]
    kv_heads = keys[0].shape[1] // HEAD
    group = heads // kv_heads
    count = len(queries)
    scores = []
    for query, key, limit in zip(queries, keys, limits):
        spread = jnp.concatenate([query] * kv_heads, axis=1) * block_mask
        score = lax.dot_general(
            spread, key, (((1,), (1,)), ((), ())), preferred_element_type=jnp.float32
        ) * (1.0 / math.sqrt(HEAD))
        column = lax.broadcasted_iota(jnp.int32, score.shape, 1)
        scores.append(jnp.where(column < limit, score, -1e30))
    scores = jnp.concatenate(scores, axis=0)
    maxima = jnp.max(scores, axis=-1, keepdims=True)
    weights = jnp.exp(scores - maxima)
    totals = jnp.sum(weights, axis=-1, keepdims=True)
    high = weights.astype(jnp.bfloat16)
    low = (weights - high.astype(jnp.float32)).astype(jnp.bfloat16)
    results = []
    for i in range(count):
        rows = slice(i * heads, (i + 1) * heads)
        both = jnp.concatenate([high[rows], low[rows]], axis=0)
        product = lax.dot_general(
            both, values[i], (((1,), (0,)), ((), ())), preferred_element_type=jnp.float32
        )
        product = product[:heads] + product[heads:]
        numerator = jnp.concatenate(
            [
                product[k * group : (k + 1) * group, k * HEAD : (k + 1) * HEAD]
                for k in range(kv_heads)
            ],
            axis=0,
        )
        results.append((numerator, maxima[rows], totals[rows]))
    return results


def kernel(
    n,
    resident,
    bounds_smem,
    queries,
    gain,
    weight,
    parents,
    lengths,
    hidden,
    step_kv,
    caches,
    out,
    prm,
    gain_v,
    weight_v,
    parent_v,
    length_v,
    rank_v,
    table_v,
    table,
    hidden_v,
    step_v,
    cache_v,
    sent_q,
    got_q,
    sent_r,
    got_r,
    sent_s,
    got_s,
    own_num,
    own_max,
    own_tot,
    part,
    other,
    small_sem,
    load_sem,
    qs_sem,
    qr_sem,
    rs_sem,
    rr_sem,
    ss_sem,
    sr_sem,
    pair_sem,
):
    me = lax.axis_index("dp")
    core = lax.axis_index("tensor")
    rows = resident * PROB
    slots = resident * resident * CAP
    heads = queries.shape[1]
    width = step_v.shape[2]
    kv_heads = width // HEAD
    group = heads // kv_heads
    beams = n * resident

    chunks = load_sem.shape[1]
    span = rows // chunks

    def load(which, chunk):
        source, target = ((step_kv, step_v), (caches, cache_v), (hidden, hidden_v))[which]
        piece = pl.ds(chunk * span, span)
        return pltpu.make_async_copy(
            source.at[piece], target.at[piece], load_sem.at[which, chunk]
        )

    small = [
        pltpu.make_async_copy(source, target, small_sem.at[i])
        for i, (source, target) in enumerate(
            ((parents, parent_v), (lengths, length_v), (gain, gain_v), (weight, weight_v))
        )
    ]
    for copy in small:
        copy.start()
    for which in range(3):
        for chunk in range(chunks):
            load(which, chunk).start()

    barrier = pltpu.get_barrier_semaphore()
    for step in range(1, n):
        pl.semaphore_signal(
            barrier, inc=1, device_id={"dp": lax.rem(me + step, n)}, device_id_type=MESH
        )
    pl.semaphore_signal(barrier, inc=1, device_id={"tensor": 1 - core}, device_id_type=MESH)

    def offset(step):
        return n // 2 + lax.div(step, 2) * (2 * lax.rem(step, 2) - 1)

    def query_copy(peer, source):
        return pltpu.make_async_remote_copy(
            src_ref=sent_q.at[peer],
            dst_ref=got_q.at[source],
            send_sem=qs_sem.at[peer],
            recv_sem=qr_sem.at[source],
            device_id={"dp": peer},
            device_id_type=MESH,
        )

    def reply_copy(peer, source):
        return pltpu.make_async_remote_copy(
            src_ref=sent_r.at[peer],
            dst_ref=got_r.at[source],
            send_sem=rs_sem.at[peer],
            recv_sem=rr_sem.at[source],
            device_id={"dp": peer},
            device_id_type=MESH,
        )

    def stat_copy(peer, source):
        return pltpu.make_async_remote_copy(
            src_ref=sent_s.at[peer],
            dst_ref=got_s.at[source],
            send_sem=ss_sem.at[peer],
            recv_sem=sr_sem.at[source],
            device_id={"dp": peer},
            device_id_type=MESH,
        )

    def pack(peer, target):
        for slot in range(slots):
            beam = slot // (resident * CAP)
            near = slot // CAP % resident
            problem = table[peer * resident + near, beam * CAP + slot % CAP]
            target[peer, slot] = queries[beam * PROB + problem]

    small[0].wait()
    small[1].wait()
    table_v[...] = jnp.zeros_like(table_v)
    parent = parent_v[...]
    problem_ids = lax.broadcasted_iota(jnp.int32, parent.shape, 1)
    beam_ids = lax.broadcasted_iota(jnp.int32, parent.shape, 0)
    rank = jnp.zeros_like(parent)
    for p in range(PROB - 1):
        sibling = (parent == parent[:, p : p + 1]) & (problem_ids > p)
        rank = rank + jnp.where(sibling, 1, 0)
    rank_v[...] = rank
    places = lax.broadcasted_iota(jnp.int32, (beams, LANES), 1)
    to_send = jnp.zeros((beams, LANES), jnp.int32)
    to_serve = jnp.zeros((beams, LANES), jnp.int32)
    live = jnp.zeros((beams, LANES), jnp.int32)
    for beam in range(resident):
        own = pl.ds(me * resident + beam, 1)
        own_parent, own_rank, own_length = parent_v[own, :], rank_v[own, :], length_v[own, :]
        for k in range(CAP):
            here = places == beam * CAP + k
            match = (own_parent == beam_ids) & (own_rank == k)
            found = jnp.sum(jnp.where(match, problem_ids, 0), axis=1, keepdims=True)
            to_send = jnp.where(here, found, to_send)
            match = (parent == me * resident + beam) & (rank == k)
            found = jnp.sum(jnp.where(match, problem_ids, 0), axis=1, keepdims=True)
            to_serve = jnp.where(here, found, to_serve)
            found = jnp.sum(jnp.where(match, own_length, 0), axis=1, keepdims=True)
            live = jnp.where(here, found, live)
    table_v[0:beams, :] = to_send
    table_v[beams : 2 * beams, :] = to_serve
    table_v[2 * beams : 3 * beams, :] = live
    table_v[3 * beams : 4 * beams, 0:PROB] = rank
    table_v[4 * beams : 5 * beams, 0:PROB] = parent
    to_scalar = pltpu.make_async_copy(table_v, table, small_sem.at[4])
    to_scalar.start()
    to_scalar.wait()

    pl.semaphore_wait(barrier, n)

    @pl.loop(1, n)
    def _(step):
        peer = lax.rem(me + offset(step), n)
        pack(peer, sent_q)
        query_copy(peer, me).start()

    pack(me, got_q)

    spread_row = lax.broadcasted_iota(jnp.int32, (heads, width), 0)
    spread_col = lax.broadcasted_iota(jnp.int32, (heads, width), 1)
    block_mask = jnp.zeros((heads, width), jnp.float32)
    for k in range(kv_heads):
        inside = (
            (spread_row >= k * group)
            & (spread_row < (k + 1) * group)
            & (spread_col >= k * HEAD)
            & (spread_col < (k + 1) * HEAD)
        )
        block_mask = jnp.where(inside, 1.0, block_mask)
    block_mask = block_mask.astype(jnp.bfloat16)
    stat_row = lax.broadcasted_iota(jnp.int32, (heads, LANES), 0)
    stat_col = lax.broadcasted_iota(jnp.int32, (heads, LANES), 1)

    for chunk in range(chunks):
        load(0, chunk).wait()
    own_batch = 8

    @pl.loop(0, rows // own_batch)
    def _(batch):
        places = [batch * own_batch + i for i in range(own_batch)]
        results = attend_group(
            [queries[j] for j in places],
            [step_v[j, :STEP, :] for j in places],
            [step_v[j, STEP:, :] for j in places],
            [bounds_smem[lax.div(j, PROB), lax.rem(j, PROB)] + 1 for j in places],
            block_mask,
        )
        for j, (numerator, maxima, totals) in zip(places, results):
            own_num[j] = numerator
            own_max[j] = jnp.broadcast_to(maxima, (heads, LANES))
            own_tot[j] = jnp.broadcast_to(totals, (heads, LANES))

    for chunk in range(chunks):
        load(1, chunk).wait()

    def serve(peer, reply, stats):
        batch = 6 if slots % 6 == 0 else slots
        for first in range(0, slots, batch):
            numbers = range(first, first + batch)
            cells = [
                (
                    peer * resident + slot // (resident * CAP),
                    slot // CAP % resident * CAP + slot % CAP,
                )
                for slot in numbers
            ]
            places = [
                slot // CAP % resident * PROB + table[beams + row, cell]
                for slot, (row, cell) in zip(numbers, cells)
            ]
            results = attend_group(
                [got_q[peer, slot] for slot in numbers],
                [cache_v[j, :CTX, :] for j in places],
                [cache_v[j, CTX:, :] for j in places],
                [table[2 * beams + row, cell] for row, cell in cells],
                block_mask,
            )
            for slot, (numerator, maxima, totals) in zip(numbers, results):
                largest = jnp.max(jnp.abs(numerator), axis=-1, keepdims=True)
                largest = jnp.maximum(largest, 1e-20)
                coded = jnp.round(numerator * (CODES / largest))
                reply[peer, slot] = coded.astype(jnp.int32).astype(jnp.int16)
                packed = jnp.where(stat_col == stat_row, maxima, 0.0)
                packed = jnp.where(stat_col == stat_row + heads, totals, packed)
                packed = jnp.where(stat_col == stat_row + 2 * heads, largest, packed)
                stats[peer, slot : slot + 1, :] = jnp.sum(packed, axis=0, keepdims=True)

    @pl.loop(1, n)
    def _(step):
        peer = lax.rem(me + n - offset(step), n)
        query_copy(peer, peer).wait_recv()
        serve(peer, sent_r, sent_s)
        reply_copy(peer, me).start()
        stat_copy(peer, me).start()

    serve(me, got_r, got_s)

    for chunk in range(chunks):
        load(2, chunk).wait()
    small[2].wait()
    small[3].wait()
    scaled = gain_v[...] * weight_v[...]
    lane = lax.broadcasted_iota(jnp.int32, (1, LANES), 1)
    last_row = jnp.zeros((1, LANES), jnp.int32)
    for j in range(rows):
        last_row = jnp.where(lane == j, bounds_smem[j // PROB, j % PROB], last_row)
    column = lax.broadcasted_iota(jnp.int32, (STEP, LANES), 1)

    def reward(j, carry):
        squares_all, products_all = carry
        wide = hidden_v[j].astype(jnp.float32)
        squares = jnp.sum(wide * wide, axis=-1, keepdims=True)
        products = jnp.sum(wide * scaled, axis=-1, keepdims=True)
        return (
            jnp.where(column == j, squares, squares_all),
            jnp.where(column == j, products, products_all),
        )

    zeros = jnp.zeros((STEP, LANES), jnp.float32)
    squares, products = lax.fori_loop(0, rows, reward, (zeros, zeros))
    part[0] = squares
    part[1] = products
    pair = pltpu.make_async_remote_copy(
        src_ref=part,
        dst_ref=other,
        send_sem=pair_sem.at[0],
        recv_sem=pair_sem.at[1],
        device_id={"tensor": 1 - core},
        device_id_type=MESH,
    )
    pair.start()
    pair.wait()
    squares = part[0] + other[0]
    products = part[1] + other[1]
    token_score = products / jnp.sqrt(squares / D_PRM + 1e-05)
    step_rows = lax.broadcasted_iota(jnp.int32, (STEP, LANES), 0)
    token_score = jnp.where(step_rows <= last_row, token_score, -1e30)
    prm[...] = jnp.max(token_score, axis=0, keepdims=True)

    @pl.loop(1, n)
    def _(step):
        peer = lax.rem(me + n - step, n)
        reply_copy(peer, peer).wait_recv()
        stat_copy(peer, peer).wait_recv()

    merge_batch = 4

    @pl.loop(0, rows // merge_batch)
    def _(batch):
        for i in range(merge_batch):
            j = batch * merge_batch + i
            beam, problem = lax.div(j, PROB), lax.rem(j, PROB)
            ancestor = table[4 * beams + me * resident + beam, problem]
            place = jnp.minimum(table[3 * beams + me * resident + beam, problem], CAP - 1)
            source = lax.div(ancestor, resident)
            slot = (beam * resident + lax.rem(ancestor, resident)) * CAP + place
            stats = got_s[source, pl.ds(slot, 1), :]
            cache_max = jnp.sum(
                jnp.where(stat_col == stat_row, stats, 0.0), axis=-1, keepdims=True
            )
            cache_tot = jnp.sum(
                jnp.where(stat_col == stat_row + heads, stats, 0.0), axis=-1, keepdims=True
            )
            cache_step = jnp.sum(
                jnp.where(stat_col == stat_row + 2 * heads, stats, 0.0), axis=-1, keepdims=True
            ) * (1.0 / CODES)
            highest = jnp.maximum(cache_max, own_max[j])
            scale_cache = jnp.exp(cache_max - highest)
            scale_own = jnp.exp(own_max[j] - highest)
            totals = cache_tot * scale_cache + own_tot[j] * scale_own
            coded = got_r[source, slot].astype(jnp.int32).astype(jnp.float32)
            cache_num = coded * (cache_step * scale_cache)
            merged = (cache_num + own_num[j] * scale_own) / totals
            out[j] = merged.astype(jnp.bfloat16)

    @pl.loop(1, n)
    def _(step):
        peer = lax.rem(me + step, n)
        query_copy(peer, me).wait_send()
        reply_copy(peer, me).wait_send()
        stat_copy(peer, me).wait_send()


def body(
    n,
    step_hidden,
    prm_gain,
    score_weight,
    step_bounds,
    queries,
    step_kv,
    caches,
    parents,
    lengths,
):
    resident = step_hidden.shape[0]
    rows = resident * PROB
    slots = resident * resident * CAP
    heads = queries.shape[-1] // HEAD
    width = caches.shape[-1]
    beams = parents.shape[0]
    smem = pl.BlockSpec(memory_space=pltpu.SMEM)
    vmem = pl.BlockSpec(memory_space=pltpu.VMEM)
    hbm = pl.BlockSpec(memory_space=pl.ANY)
    chunks = 4
    dma = pltpu.SemaphoreType.DMA
    attended, prm = pl.pallas_call(
        functools.partial(kernel, n, resident),
        out_shape=(
            jax.ShapeDtypeStruct((rows, heads, HEAD), jnp.bfloat16),
            jax.ShapeDtypeStruct((1, LANES), jnp.float32),
        ),
        in_specs=[smem, vmem] + [hbm] * 7,
        out_specs=(vmem, vmem),
        scratch_shapes=[
            pltpu.VMEM((1, prm_gain.shape[0]), jnp.float32),
            pltpu.VMEM((1, prm_gain.shape[0]), jnp.float32),
            pltpu.VMEM((beams, PROB), jnp.int32),
            pltpu.VMEM((beams, PROB), jnp.int32),
            pltpu.VMEM((beams, PROB), jnp.int32),
            pltpu.VMEM((5 * beams, LANES), jnp.int32),
            pltpu.SMEM((5 * beams, LANES), jnp.int32),
            pltpu.VMEM((rows, STEP, step_hidden.shape[-1]), jnp.bfloat16),
            pltpu.VMEM((rows, 2 * STEP, width), jnp.bfloat16),
            pltpu.VMEM((rows, 2 * CTX, width), jnp.bfloat16),
            pltpu.VMEM((n, slots, heads, HEAD), jnp.bfloat16),
            pltpu.VMEM((n, slots, heads, HEAD), jnp.bfloat16),
            pltpu.VMEM((n, slots, heads, HEAD), jnp.int16),
            pltpu.VMEM((n, slots, heads, HEAD), jnp.int16),
            pltpu.VMEM((n, -(-slots // 8) * 8, LANES), jnp.float32),
            pltpu.VMEM((n, -(-slots // 8) * 8, LANES), jnp.float32),
            pltpu.VMEM((rows, heads, HEAD), jnp.float32),
            pltpu.VMEM((rows, heads, LANES), jnp.float32),
            pltpu.VMEM((rows, heads, LANES), jnp.float32),
            pltpu.VMEM((2, STEP, LANES), jnp.float32),
            pltpu.VMEM((2, STEP, LANES), jnp.float32),
            dma((5,)),
            dma((3, chunks)),
            dma((n,)),
            dma((n,)),
            dma((n,)),
            dma((n,)),
            dma((n,)),
            dma((n,)),
            dma((2,)),
        ],
        compiler_params=pltpu.CompilerParams(
            collective_id=0, has_side_effects=True, vmem_limit_bytes=54400 * 1024
        ),
    )(
        step_bounds,
        queries.reshape(rows, heads, HEAD),
        prm_gain.reshape(1, -1),
        score_weight.reshape(1, -1),
        parents[:, :, 0],
        lengths,
        step_hidden.reshape(rows, STEP, step_hidden.shape[-1]),
        step_kv.reshape(rows, 2 * STEP, width),
        caches.reshape(rows, 2 * CTX, width),
    )
    attended = attended.reshape(resident, PROB, heads * HEAD)
    return attended, prm[0, :rows].reshape(resident, PROB)


def solution(mesh):
    in_specs = (
        P("dp", "groups", None, "tensor"),
        P("tensor"),
        P("tensor"),
        P("dp", "groups"),
        P("dp", "groups", "tensor"),
        P("dp", "groups", None, None, "tensor"),
        P("dp", "groups", None, None, "tensor"),
        P(None, "groups", None),
        P(None, "groups"),
    )
    out_specs = (P("dp", "groups", "tensor"), P("dp", "groups"))
    return jax.shard_map(
        functools.partial(body, mesh.shape["dp"]),
        mesh=mesh,
        in_specs=in_specs,
        out_specs=out_specs,
        check_vma=False,
    )
```
